32 devices in a mesh: feat: 16 (over z, x, core), dp: 2 (over y).
Axes of the slice: x: 2, y: 2, z: 4, core: 2. Of those that a mesh axis runs over, the one named last changes fastest.
Arguments:
- x_feat: bfloat16 [2, 1024, 26624], P('dp', 'feat'), may hold values from -6 to 6
- tiles_one: bfloat16 [2, 64, 128, 128], P('dp', 'feat'), may hold values from 0 to 0.13183594
- tile_cols: int32 [2, 64], P('dp', 'feat'), may hold values from 0 to 207
- tile_counts: int32 [2, 16], P('dp', 'feat'), may hold values from 1 to 4, as said below
- w_one: bfloat16 [2, 1024, 256], P(None, 'feat'), may hold values from -0.1875 to 0.1875
- b_one: float32 [256], replicated, may hold values from -3 to 3
- adj_two: bfloat16 [2, 2048, 128], P('dp', 'feat'), may hold values from 0 to 0.03125
- w_two: bfloat16 [2, 256, 256], replicated, may hold values from -0.375 to 0.375
- b_two: float32 [256], replicated, may hold values from -3 to 3
- cotangent: bfloat16 [2, 2048, 256], P('dp', 'feat'), may hold values from -0.09375 to 0.09375
Outputs:
- out_two: bfloat16 [2, 2048, 256], P('dp', 'feat')
- grad_w_one: float32 [2, 1024, 256], P(None, 'feat')
- grad_b_one: float32 [256], replicated
- grad_w_two: float32 [2, 256, 256], replicated
- grad_b_two: float32 [256], replicated
The draws below stay inside these ranges and needn't reach their ends.
Inputs may be any that keep to these rules, and one draw needn't show every extreme that they name: `tile_counts`: the first 2048 source nodes are the minibatch's nodes themselves; in every replica some row block has all 4 slots live.
All inputs are finite; a program needn't handle non-finite values.
Results may differ from the reference program's by a relative error of at most 0.0085.
Values may be sent and summed in bfloat16 or wider, within the bound.
A program may use at most 64 MiB of HBM per device.

```python
import jax
import jax.numpy as jnp

F = 1024
HID = 256
OUT = 256
TILE = 128
CAP1 = 4
BLOCKS = 16
REPLICAS = 2
N1 = 2048
SRC_BLK = 208
N0 = 26624
SLOTS = 64
ROWS = 4096


def draw_tile_counts(key, part):
    key = jax.random.fold_in(key, 11)
    key_vals, key_pos = jax.random.split(key)
    counts = jax.random.randint(key_vals, (REPLICAS, BLOCKS), 1, CAP1 + 1)
    full_at = jax.random.randint(key_pos, (REPLICAS, 1), 0, BLOCKS)
    full = jnp.arange(BLOCKS)[None, :] == full_at
    return jnp.where(full, CAP1, counts).astype(jnp.int32)


def place_ends(entries, key, smallest, largest):
    shape = entries.shape
    index_at = [jax.random.randint(jax.random.fold_in(key, axis), (), 0, shape[axis]) for axis in range(len(shape))]
    entries = entries.at[tuple(index_at)].set(smallest)
    longest = shape.index(max(shape))
    index_at[longest] = (index_at[longest] + 1) % shape[longest]
    return entries.at[tuple(index_at)].set(largest)


def shard_levels(rng, shape, pieces, low, largest):
    def one(axis_at, blocks):
        heights = jax.random.uniform(jax.random.fold_in(jax.random.fold_in(rng, 6), axis_at), (blocks,), jnp.float32, low / len(pieces), largest / len(pieces))
        return jnp.repeat(jnp.exp(heights), shape[axis_at] // blocks).reshape((-1,) + (1,) * (len(shape) - axis_at - 1))

    gain = one(*pieces[0])
    for cut in pieces[1:]:
        gain = gain * one(*cut)
    return gain


def scatter_about(key, dims, deviation, limit, pieces=(), dtype=jnp.bfloat16):
    loudness = shard_levels(key, dims, pieces, -0.22, 0.18) if pieces else 1.0
    result = jax.random.normal(key, dims, jnp.float32) * deviation * loudness
    return jnp.minimum(jnp.maximum(result, -limit), limit).astype(dtype)


def setup_inputs(seed: int = 0) -> dict:
    seeds = jax.random.split(jax.random.key(seed), 11)
    x_feat = scatter_about(seeds[0], (REPLICAS, F, N0), 1.0, 6.0, ((0, 2), (1, 16)))
    tiles_one = jnp.clip(0.13183594 * jax.random.uniform(seeds[1], (REPLICAS, SLOTS, TILE, TILE), jnp.float32) ** shard_levels(seeds[1], (REPLICAS, SLOTS, TILE, TILE), ((0, 2), (1, 16)), -0.2, 0.2), 0.0, 0.13183594).astype(jnp.bfloat16)
    tile_cols = place_ends(jax.random.randint(seeds[2], (REPLICAS, SLOTS), 0, SRC_BLK), jax.random.fold_in(seeds[2], 1), 0, SRC_BLK - 1).astype(jnp.int32)
    tile_counts = draw_tile_counts(jax.random.fold_in(seeds[10], 71), 0)
    w_one = scatter_about(seeds[4], (2, F, HID), F ** -0.5, 0.1875, ((1, 16),))
    b_one = scatter_about(seeds[5], (HID,), 0.5, 3.0, (), jnp.float32)
    adj_two = jnp.clip(0.03125 * jax.random.uniform(seeds[6], (REPLICAS, N1, TILE), jnp.float32) ** shard_levels(seeds[6], (REPLICAS, N1, TILE), ((0, 2), (1, 16)), -0.2, 0.2), 0.0, 0.03125).astype(jnp.bfloat16)
    w_two = scatter_about(seeds[7], (2, HID, OUT), HID ** -0.5, 0.375)
    b_two = scatter_about(seeds[8], (OUT,), 0.5, 3.0, (), jnp.float32)
    cotangent = scatter_about(seeds[9], (REPLICAS, N1, OUT), (1.0 / ROWS ** 0.5), 0.09375, ((0, 2), (1, 16)))
    return {"x_feat": x_feat, "tiles_one": tiles_one, "tile_cols": tile_cols, "tile_counts": tile_counts, "w_one": w_one, "b_one": b_one, "adj_two": adj_two, "w_two": w_two, "b_two": b_two, "cotangent": cotangent}


def reference(x_feat, tiles_one, tile_cols, tile_counts, w_one, b_one, adj_two, w_two, b_two, cotangent):
    outs = []
    grad_w1 = jnp.zeros((2, F, HID), jnp.float32)
    grad_b1 = jnp.zeros((HID,), jnp.float32)
    grad_w2 = jnp.zeros((2, HID, OUT), jnp.float32)
    grad_b2 = jnp.zeros((OUT,), jnp.float32)
    for rep in range(REPLICAS):
        feats = x_feat[rep]
        blocks = feats.reshape(F, SRC_BLK, TILE)
        picked = jnp.take(blocks, tile_cols[rep], axis=1)
        slot_live = (jnp.arange(SLOTS) % CAP1 < jnp.repeat(tile_counts[rep], CAP1)).astype(jnp.float32)
        contrib = jnp.einsum("fst,sut->fsu", picked.astype(jnp.float32), tiles_one[rep].astype(jnp.float32))
        contrib = contrib * slot_live[None, :, None]
        agg_one = contrib.reshape(F, BLOCKS, CAP1, TILE).sum(axis=2).reshape(F, N1).astype(jnp.bfloat16)
        x_self = feats[:, :N1]
        z_one = jnp.dot(x_self.T, w_one[0], preferred_element_type=jnp.float32)
        z_one = z_one + jnp.dot(agg_one.T, w_one[1], preferred_element_type=jnp.float32) + b_one
        h_one = jax.nn.silu(z_one).astype(jnp.bfloat16)
        adj_blocks = adj_two[rep].reshape(BLOCKS, TILE, TILE).astype(jnp.float32)
        h_blocks = h_one.reshape(BLOCKS, TILE, HID).astype(jnp.float32)
        agg_two = jnp.einsum("pij,pjh->pih", adj_blocks, h_blocks).reshape(N1, HID).astype(jnp.bfloat16)
        z_two = jnp.dot(h_one, w_two[0], preferred_element_type=jnp.float32)
        z_two = z_two + jnp.dot(agg_two, w_two[1], preferred_element_type=jnp.float32) + b_two
        outs.append(z_two.astype(jnp.bfloat16))
        grad_out = cotangent[rep]
        grad_w2 = grad_w2 + jnp.stack([jnp.dot(h_one.T, grad_out, preferred_element_type=jnp.float32), jnp.dot(agg_two.T, grad_out, preferred_element_type=jnp.float32)])
        grad_b2 = grad_b2 + jnp.sum(grad_out.astype(jnp.float32), axis=0)
        dagg_two = jnp.dot(grad_out, w_two[1].T, preferred_element_type=jnp.float32).astype(jnp.bfloat16)
        dagg_blocks = dagg_two.reshape(BLOCKS, TILE, HID).astype(jnp.float32)
        dh_one = jnp.dot(grad_out, w_two[0].T, preferred_element_type=jnp.float32)
        dh_one = dh_one + jnp.einsum("pji,pjh->pih", adj_blocks, dagg_blocks).reshape(N1, HID)
        sig = jax.nn.sigmoid(z_one)
        dz_one = (dh_one * sig * (1.0 + z_one * (1.0 - sig))).astype(jnp.bfloat16)
        grad_w1 = grad_w1 + jnp.stack([jnp.dot(x_self, dz_one, preferred_element_type=jnp.float32), jnp.dot(agg_one, dz_one, preferred_element_type=jnp.float32)])
        grad_b1 = grad_b1 + jnp.sum(dz_one.astype(jnp.float32), axis=0)
    return jnp.stack(outs), grad_w1, grad_b1, grad_w2, grad_b2
```

```python
import functools
import math

import jax
import jax.numpy as jnp
from jax import lax
from jax.experimental import pallas as pl
from jax.experimental.pallas import tpu as pltpu
from jax.sharding import PartitionSpec as P

BF = jnp.bfloat16
F32 = jnp.float32


def dot(a, b, dims=((1,), (0,))):
    return lax.dot_general(a, b, (dims, ((), ())), preferred_element_type=F32)


def grid_of(n):
    x = max(math.isqrt(n // 4), 1)
    while (n // 2) % x:
        x -= 1
    return n // 2 // x, x


def kernel(
    n, dp, zs, xs,
    x_hbm, tiles, cols, counts, w1, b1, adj, w2, b2, cot,
    out2, gw1, gb1, gw2, gb2,
    xv, pack, mv, agg, dzb, colv, coli, cols_s, dh_s, acc,
    w2s, w2r, g2s, g2r, bs, bb, dps, dpr, w1s, w1r,
    ag_send, ag_recv, dz_send, dz_recv, pair_sem, loc_sem,
):
    me = lax.axis_index("feat")
    my_dp = lax.axis_index("dp")
    core = lax.rem(me, 2)
    chip = lax.div(me, 2)
    xx = lax.rem(chip, xs)
    zz = lax.div(chip, xs)
    sl = w1.shape[1]
    tile = adj.shape[0]
    slots = tiles.shape[0]
    trows = slots * tile
    hid = w1.shape[2]
    half_w = hid // 2
    rows = w2s.shape[1]

    def index(z, x, c):
        return (z * xs + x) * 2 + c

    def remote(src, dst, ssem, rsem, peer, axis="feat"):
        return pltpu.make_async_remote_copy(
            src_ref=src, dst_ref=dst, send_sem=ssem, recv_sem=rsem,
            device_id={axis: peer}, device_id_type=pl.DeviceIdType.MESH,
        )

    def wait_for(ref, sem):
        pltpu.make_async_copy(ref, ref, sem).wait()

    @pl.loop(0, xv.shape[0])
    def _(b):
        at = pl.multiple_of(b * tile, tile)
        pltpu.make_async_copy(x_hbm.at[:, pl.ds(at, tile)], xv.at[b], loc_sem.at[0]).start()

    barrier = pltpu.get_barrier_semaphore()

    @pl.loop(1, n)
    def _(k):
        pl.semaphore_signal(
            barrier, inc=1, device_id={"feat": lax.rem(me + k, n)}, device_id_type=pl.DeviceIdType.MESH
        )

    @pl.loop(1, dp)
    def _(k):
        pl.semaphore_signal(
            barrier, inc=1, device_id={"dp": lax.rem(my_dp + k, dp)}, device_id_type=pl.DeviceIdType.MESH
        )

    count = counts[0, 0]
    lane = lax.broadcasted_iota(jnp.int32, (1, 128), 1)
    info = jnp.zeros((1, 128), jnp.int32)
    for s in range(slots):
        live = jnp.minimum(jnp.maximum(count - s, 0), 1).astype(F32)
        pack[me, s * tile : (s + 1) * tile, :] = (tiles[s].astype(F32) * live).astype(BF)
        info = jnp.where(lane == s, cols[0, s], info)
    colv[...] = info
    for k in range(2):
        for h in range(2):
            at = trows + (k * 2 + h) * sl
            pack[me, at : at + sl, :] = w1[k, :, h * half_w : (h + 1) * half_w]
    bs[...] = jnp.zeros_like(bs)
    bs[1:2, :] = jnp.sum(cot[...].astype(F32), axis=0, keepdims=True)
    pl.semaphore_wait(barrier, n - 1 + dp - 1)

    class Gather:
        def __init__(self, buf, send, recv):
            self.buf, self.send, self.recv = buf, send, recv
            self.half = buf.shape[1] // 2

        def view(self, h, src):
            return self.buf.at[src, pl.ds(h * self.half, self.half), :]

        def copy(self, h, src, slot, peer):
            v = self.view(h, src)
            return remote(v, v, self.send.at[h, src, slot], self.recv.at[h, src], peer)

        def wait(self, h, src):
            wait_for(self.view(h, src), self.recv.at[h, src])

        def up(self, h, src, act):
            @pl.when(zz < zs - 1)
            def _():
                act(self.copy(h, src, 0, index(zz + 1, xx, core)))

        def down(self, h, src, act):
            @pl.when(zz > 0)
            def _():
                act(self.copy(h, src, 1, index(zz - 1, xx, core)))

        def across(self, h, src, act):
            for k in range(1, xs):
                act(self.copy(h, src, 1 + k, index(zz, lax.rem(xx + k, xs), core)))

        def sibling(self, h, src, act):
            act(self.copy(h, src, xs + 1, index(zz, xx, 1 - core)))

        def walk(self, act, first, arrive):
            for h in (1, 0):
                self.across(h, me, act)
                self.up(h, me, act)
                self.down(h, me, act)
                self.sibling(h, me, act)
            first()
            for k in range(1, xs):
                src = index(zz, lax.rem(xx + k, xs), core)
                arrive(1, src)
                self.up(1, src, act)
                self.down(1, src, act)
                self.sibling(1, src, act)

            @pl.loop(1, zs)
            def _(k):
                @pl.when(zz - k >= 0)
                def _():
                    src = index(zz - k, xx, core)
                    arrive(0, src)
                    self.up(0, src, act)
                    self.across(0, src, act)
                    self.sibling(0, src, act)

                @pl.when(zz + k < zs)
                def _():
                    src = index(zz + k, xx, core)
                    arrive(0, src)
                    self.down(0, src, act)
                    self.across(0, src, act)
                    self.sibling(0, src, act)

                for j in range(xs):
                    other = lax.rem(xx + j, xs)

                    @pl.when(zz - k >= 0)
                    def _():
                        src = index(zz - k, other, core)
                        arrive(1, src)
                        self.up(1, src, act)
                        self.sibling(1, src, act)

                    @pl.when(zz + k < zs)
                    def _():
                        src = index(zz + k, other, core)
                        arrive(1, src)
                        self.down(1, src, act)
                        self.sibling(1, src, act)

            @pl.loop(0, zs)
            def _(k):
                z = lax.rem(zz + k, zs)
                for j in range(1, xs):
                    src = index(z, lax.rem(xx + j, xs), core)
                    arrive(0, src)
                    self.sibling(0, src, act)

        def run(self, first):
            self.walk(lambda c: c.start(), first, self.wait)

        def finish(self):
            self.walk(lambda c: c.wait_send(), lambda: None, lambda h, s: None)

    def backward_start():
        dagg = dot(cot[...], w2[1], ((1,), (1,))).astype(BF)
        dh = dot(cot[...], w2[0], ((1,), (1,)))
        dh_s[...] = dh + dot(adj[...], dagg, ((0,), (0,)))

    def features_out():
        wait_for(xv, loc_sem.at[0])

        @pl.loop(1, n)
        def _(k):
            p = lax.rem(me + k, n)
            remote(
                xv.at[p], mv.at[0, me], pair_sem.at[2], pair_sem.at[3], p,
            ).start()

        pltpu.make_async_copy(
            xv.at[me], mv.at[0, me], pair_sem.at[3]
        ).start()

    @pl.loop(1, n)
    def _(k):
        remote(colv, coli.at[me], pair_sem.at[0], pair_sem.at[1], lax.rem(me + k, n)).start()

    pltpu.make_async_copy(colv, coli.at[me], pair_sem.at[1]).start()

    def before_relay():
        features_out()
        backward_start()

    gather = Gather(pack, ag_send, ag_recv)
    gather.run(before_relay)
    wait_for(coli, pair_sem.at[1])
    to_smem = pltpu.make_async_copy(coli, cols_s, loc_sem.at[1])
    to_smem.start()
    to_smem.wait()

    def aggregate(r):
        total = jnp.zeros((sl, tile), F32)
        for s in range(slots):
            total += dot(xv[cols_s[r, 0, s]], pack[r, s * tile : (s + 1) * tile, :], ((1,), (1,)))
        agg[r] = total.astype(BF)

        @pl.when(r != me)
        def _():
            remote(agg.at[r], mv.at[1, me], pair_sem.at[4], pair_sem.at[5], r).start()

        @pl.when(r == me)
        def _():
            pltpu.make_async_copy(agg.at[r], mv.at[1, me], pair_sem.at[5]).start()

    half_n = n // 2

    @pl.loop(0, half_n)
    def _(j):
        aggregate(lax.rem(chip + j, half_n) * 2 + core)

    @pl.loop(0, half_n)
    def _(j):
        r = lax.rem(chip + j, half_n) * 2 + 1 - core
        gather.wait(0, r)
        gather.wait(1, r)
        aggregate(r)

    def project(k):
        at = trows + k * 2 * sl
        w = jnp.concatenate(
            [
                pack[:, at + h * sl : at + (h + 1) * sl, :].reshape(n * sl, half_w)
                for h in range(2)
            ],
            axis=1,
        )
        return dot(mv[k].reshape(n * sl, tile), w, ((0,), (0,)))

    wait_for(mv.at[0], pair_sem.at[3])
    acc[...] = project(0) + b1[...]
    wait_for(mv.at[1], pair_sem.at[5])
    z = acc[...] + project(1)
    sig = 1.0 / (1.0 + jnp.exp(-z))
    h_one = (z * sig).astype(BF)
    dz = (dh_s[...] * sig * (1.0 + z * (1.0 - sig))).astype(BF)
    dzb[me] = dz
    bs[0:1, :] = jnp.sum(dz.astype(F32), axis=0, keepdims=True)

    def forward():
        agg_two = dot(adj[...], h_one).astype(BF)
        g0 = dot(h_one, cot[...], ((0,), (0,)))
        g1 = dot(agg_two, cot[...], ((0,), (0,)))
        w2s[: n // 2] = g0.reshape(n // 2, rows, hid).astype(w2s.dtype)
        w2s[n // 2 :] = g1.reshape(n // 2, rows, hid).astype(w2s.dtype)

        @pl.loop(1, n)
        def _(k):
            p = lax.rem(me + k, n)
            remote(w2s.at[p], w2r.at[me], pair_sem.at[6], pair_sem.at[7], p).start()
            remote(bs, bb.at[me], pair_sem.at[8], pair_sem.at[9], p).start()

        pltpu.make_async_copy(w2s.at[me], w2r.at[me], pair_sem.at[7]).start()
        pltpu.make_async_copy(bs, bb.at[me], pair_sem.at[9]).start()
        z2 = dot(h_one, w2[0]) + dot(agg_two, w2[1]) + b2[...]
        out2[...] = z2.astype(BF)

    dgather = Gather(dzb, dz_send, dz_recv)
    dgather.run(forward)

    wait_for(w2r, pair_sem.at[7])
    wait_for(bb, pair_sem.at[9])
    dps[0:rows, :] = jnp.sum(w2r[...].astype(F32), axis=0)
    dps[rows:, :] = jnp.sum(bb[...], axis=0)

    def over_replicas(src, dst, ssem, rsem):
        @pl.loop(1, dp)
        def _(k):
            remote(src, dst.at[my_dp], ssem, rsem, lax.rem(my_dp + k, dp), "dp").start()

        pltpu.make_async_copy(src, dst.at[my_dp], rsem).start()

    over_replicas(dps, dpr, pair_sem.at[10], pair_sem.at[11])

    acc[...] = jnp.zeros_like(acc)

    def weight(r):
        lhs = jnp.concatenate([xv[r], agg[r]], axis=0)
        acc[0 : 2 * sl, :] += dot(lhs, dzb[r])

    @pl.loop(0, half_n)
    def _(j):
        weight(lax.rem(chip + j, half_n) * 2 + core)

    wait_for(dpr, pair_sem.at[11])
    total = dpr[0]
    for k in range(1, dp):
        total = total + dpr[k]
    g2s[...] = total[0:rows].astype(g2s.dtype)
    gb1[...] = total[rows : rows + 1]
    gb2[...] = total[rows + 1 : rows + 2]

    @pl.loop(1, n)
    def _(k):
        remote(g2s, g2r.at[me], pair_sem.at[12], pair_sem.at[13], lax.rem(me + k, n)).start()

    pltpu.make_async_copy(g2s, g2r.at[me], pair_sem.at[13]).start()

    @pl.loop(0, half_n)
    def _(j):
        r = lax.rem(chip + j, half_n) * 2 + 1 - core
        dgather.wait(0, r)
        dgather.wait(1, r)
        weight(r)

    w1s[...] = acc[0 : 2 * sl, :].astype(w1s.dtype)
    over_replicas(w1s, w1r, pair_sem.at[14], pair_sem.at[15])
    gather.finish()
    dgather.finish()

    def sent(ref, sem):
        wait_for(ref, sem)

    sent(coli.at[pl.ds(0, n - 1)], pair_sem.at[0])
    sent(mv.at[0, pl.ds(0, n - 1)], pair_sem.at[2])
    sent(mv.at[1, pl.ds(0, n - 1)], pair_sem.at[4])
    sent(w2r.at[pl.ds(0, n - 1)], pair_sem.at[6])
    sent(bb.at[pl.ds(0, n - 1)], pair_sem.at[8])
    wait_for(g2r, pair_sem.at[13])
    gw2[...] = g2r[...].astype(F32).reshape(n * rows, hid)
    sent(g2r.at[pl.ds(0, n - 1)], pair_sem.at[12])
    if dp > 1:
        sent(dpr.at[pl.ds(0, dp - 1)], pair_sem.at[10])
    wait_for(w1r, pair_sem.at[15])
    total = w1r[0].astype(F32)
    for k in range(1, dp):
        total = total + w1r[k].astype(F32)
    gw1[...] = total
    if dp > 1:
        sent(w1r.at[pl.ds(0, dp - 1)], pair_sem.at[14])


def local(n, dp, x_feat, tiles_one, tile_cols, tile_counts, w_one, b_one, adj_two, w_two, b_two, cotangent):
    zs, xs = grid_of(n)
    sl, width = x_feat.shape[1:]
    tile = adj_two.shape[-1]
    slots = tiles_one.shape[1]
    hid = w_one.shape[2]
    rows = 2 * hid // n
    narrow = BF if rows % 16 == 0 else F32
    packed = slots * tile + 4 * sl
    vmem = pl.BlockSpec(memory_space=pltpu.VMEM)
    smem = pl.BlockSpec(memory_space=pltpu.SMEM)
    dma = pltpu.SemaphoreType.DMA
    out2, gw1, gb1, gw2, gb2 = pl.pallas_call(
        functools.partial(kernel, n, dp, zs, xs),
        out_shape=(
            jax.ShapeDtypeStruct((tile, hid), BF),
            jax.ShapeDtypeStruct((2 * sl, hid), F32),
            jax.ShapeDtypeStruct((1, hid), F32),
            jax.ShapeDtypeStruct((2 * hid, hid), F32),
            jax.ShapeDtypeStruct((1, hid), F32),
        ),
        in_specs=[
            pl.BlockSpec(memory_space=pl.ANY), vmem, smem, smem, vmem, vmem, vmem, vmem, vmem, vmem,
        ],
        out_specs=(vmem,) * 5,
        scratch_shapes=[
            pltpu.VMEM((width // tile, sl, tile), BF),
            pltpu.VMEM((n, packed, tile), BF),
            pltpu.VMEM((2, n, sl, tile), BF),
            pltpu.VMEM((n, sl, tile), BF),
            pltpu.VMEM((n, tile, hid), BF),
            pltpu.VMEM((1, 128), jnp.int32),
            pltpu.VMEM((n, 1, 128), jnp.int32),
            pltpu.SMEM((n, 1, 128), jnp.int32),
            pltpu.VMEM((tile, hid), F32),
            pltpu.VMEM((max(tile, 2 * sl), hid), F32),
            pltpu.VMEM((n, rows, hid), narrow),
            pltpu.VMEM((n, rows, hid), narrow),
            pltpu.VMEM((rows, hid), narrow),
            pltpu.VMEM((n, rows, hid), narrow),
            pltpu.VMEM((8, hid), F32),
            pltpu.VMEM((n, 8, hid), F32),
            pltpu.VMEM((rows + 8, hid), F32),
            pltpu.VMEM((dp, rows + 8, hid), F32),
            pltpu.VMEM((2 * sl, hid), BF),
            pltpu.VMEM((dp, 2 * sl, hid), BF),
            dma((2, n, xs + 2)),
            dma((2, n)),
            dma((2, n, xs + 2)),
            dma((2, n)),
            dma((16,)),
            dma((2,)),
        ],
        compiler_params=pltpu.CompilerParams(
            collective_id=0, has_side_effects=True, vmem_limit_bytes=48 * 1024 * 1024
        ),
    )(
        x_feat[0], tiles_one[0], tile_cols, tile_counts, w_one, b_one[None], adj_two[0], w_two,
        b_two[None], cotangent[0],
    )
    return (
        out2[None], gw1.reshape(2, sl, hid), gb1[0], gw2.reshape(2, hid, hid), gb2[0],
    )


def solution(mesh):
    in_specs = (
        P("dp", "feat", None),
        P("dp", "feat", None, None),
        P("dp", "feat"),
        P("dp", "feat"),
        P(None, "feat", None),
        P(),
        P("dp", "feat", None),
        P(),
        P(),
        P("dp", "feat", None),
    )
    out_specs = (P("dp", "feat", None), P(None, "feat", None), P(), P(), P())
    return jax.shard_map(
        functools.partial(local, mesh.shape["feat"], mesh.shape["dp"]),
        mesh=mesh, in_specs=in_specs, out_specs=out_specs, check_vma=False,
    )
```

```python
import functools
import math

import jax
import jax.numpy as jnp
from jax import lax
from jax.experimental import pallas as pl
from jax.experimental.pallas import tpu as pltpu
from jax.sharding import PartitionSpec as P

BF = jnp.bfloat16
F32 = jnp.float32


def dot(a, b, dims=((1,), (0,))):
    return lax.dot_general(a, b, (dims, ((), ())), preferred_element_type=F32)


def grid_of(n):
    x = max(math.isqrt(n // 4), 1)
    while (n // 2) % x:
        x -= 1
    return n // 2 // x, x


def kernel(
    n, dp, zs, xs,
    x_hbm, tiles_h, cols_h, counts_h, w1_h, b1_h, adj_h, w2_h, b2_h, cot_h,
    out2, gw1, gb1, gw2, gb2,
    xv, pack, mv, agg, dzb, colv, coli, cols_s, dh_s, acc,
    w2s, w2r, g2s, g2r, bs, bb, dps, dpr, w1s, w1r,
    tiles, cols, counts, w1, b1, adj, w2, b2, cot,
    ag_send, ag_recv, dz_send, dz_recv, pair_sem, loc_sem,
):
    me = lax.axis_index("feat")
    my_dp = lax.axis_index("dp")
    core = lax.rem(me, 2)
    chip = lax.div(me, 2)
    xx = lax.rem(chip, xs)
    zz = lax.div(chip, xs)
    sl = w1.shape[1]
    tile = adj.shape[0]
    slots = tiles.shape[0]
    trows = slots * tile
    hid = w1.shape[2]
    half_w = hid // 2
    rows = w2s.shape[1]

    def index(z, x, c):
        return (z * xs + x) * 2 + c

    def remote(src, dst, ssem, rsem, peer, axis="feat"):
        return pltpu.make_async_remote_copy(
            src_ref=src, dst_ref=dst, send_sem=ssem, recv_sem=rsem,
            device_id={axis: peer}, device_id_type=pl.DeviceIdType.MESH,
        )

    def wait_for(ref, sem):
        pltpu.make_async_copy(ref, ref, sem).wait()

    early = [
        pltpu.make_async_copy(src, dst, loc_sem.at[2 + k])
        for k, (src, dst) in enumerate(
            [
                (cols_h, cols), (counts_h, counts), (tiles_h, tiles), (w1_h, w1), (cot_h, cot),
                (w2_h, w2), (adj_h, adj), (b1_h, b1), (b2_h, b2),
            ]
        )
    ]
    for copy in early:
        copy.start()
    barrier = pltpu.get_barrier_semaphore()

    @pl.loop(1, n)
    def _(k):
        pl.semaphore_signal(
            barrier, inc=1, device_id={"feat": lax.rem(me + k, n)}, device_id_type=pl.DeviceIdType.MESH
        )

    @pl.loop(1, dp)
    def _(k):
        pl.semaphore_signal(
            barrier, inc=1, device_id={"dp": lax.rem(my_dp + k, dp)}, device_id_type=pl.DeviceIdType.MESH
        )

    @pl.loop(0, xv.shape[0])
    def _(b):
        at = pl.multiple_of(b * tile, tile)
        pltpu.make_async_copy(x_hbm.at[:, pl.ds(at, tile)], xv.at[b], loc_sem.at[0]).start()

    for copy in early:
        copy.wait()
    count = counts[0, 0]
    lane = lax.broadcasted_iota(jnp.int32, (1, 128), 1)
    info = jnp.zeros((1, 128), jnp.int32)
    for s in range(slots):
        live = jnp.minimum(jnp.maximum(count - s, 0), 1).astype(F32)
        pack[me, s * tile : (s + 1) * tile, :] = (tiles[s].astype(F32) * live).astype(BF)
        info = jnp.where(lane == s, cols[0, s], info)
    colv[...] = info
    for k in range(2):
        for h in range(2):
            at = trows + (k * 2 + h) * sl
            pack[me, at : at + sl, :] = w1[k, :, h * half_w : (h + 1) * half_w]
    bs[...] = jnp.zeros_like(bs)
    bs[1:2, :] = jnp.sum(cot[...].astype(F32), axis=0, keepdims=True)
    pl.semaphore_wait(barrier, n - 1 + dp - 1)

    class Gather:
        def __init__(self, buf, send, recv):
            self.buf, self.send, self.recv = buf, send, recv
            self.half = buf.shape[1] // 2

        def view(self, h, src):
            return self.buf.at[src, pl.ds(h * self.half, self.half), :]

        def copy(self, h, src, slot, peer):
            v = self.view(h, src)
            return remote(v, v, self.send.at[h, src, slot], self.recv.at[h, src], peer)

        def wait(self, h, src):
            wait_for(self.view(h, src), self.recv.at[h, src])

        def up(self, h, src, act):
            @pl.when(zz < zs - 1)
            def _():
                act(self.copy(h, src, 0, index(zz + 1, xx, core)))

        def down(self, h, src, act):
            @pl.when(zz > 0)
            def _():
                act(self.copy(h, src, 1, index(zz - 1, xx, core)))

        def across(self, h, src, act):
            for k in range(1, xs):
                act(self.copy(h, src, 1 + k, index(zz, lax.rem(xx + k, xs), core)))

        def sibling(self, h, src, act):
            act(self.copy(h, src, xs + 1, index(zz, xx, 1 - core)))

        def walk(self, act, first, arrive):
            for h in (1, 0):
                self.across(h, me, act)
                self.up(h, me, act)
                self.down(h, me, act)
                self.sibling(h, me, act)
            first()
            for k in range(1, xs):
                src = index(zz, lax.rem(xx + k, xs), core)
                arrive(1, src)
                self.up(1, src, act)
                self.down(1, src, act)
                self.sibling(1, src, act)

            @pl.loop(1, zs)
            def _(k):
                @pl.when(zz - k >= 0)
                def _():
                    src = index(zz - k, xx, core)
                    arrive(0, src)
                    self.up(0, src, act)
                    self.across(0, src, act)
                    self.sibling(0, src, act)

                @pl.when(zz + k < zs)
                def _():
                    src = index(zz + k, xx, core)
                    arrive(0, src)
                    self.down(0, src, act)
                    self.across(0, src, act)
                    self.sibling(0, src, act)

                for j in range(xs):
                    other = lax.rem(xx + j, xs)

                    @pl.when(zz - k >= 0)
                    def _():
                        src = index(zz - k, other, core)
                        arrive(1, src)
                        self.up(1, src, act)
                        self.sibling(1, src, act)

                    @pl.when(zz + k < zs)
                    def _():
                        src = index(zz + k, other, core)
                        arrive(1, src)
                        self.down(1, src, act)
                        self.sibling(1, src, act)

            @pl.loop(0, zs)
            def _(k):
                z = lax.rem(zz + k, zs)
                for j in range(1, xs):
                    src = index(z, lax.rem(xx + j, xs), core)
                    arrive(0, src)
                    self.sibling(0, src, act)

        def run(self, first):
            self.walk(lambda c: c.start(), first, self.wait)

        def finish(self):
            self.walk(lambda c: c.wait_send(), lambda: None, lambda h, s: None)

    def backward_start():
        dagg = dot(cot[...], w2[1], ((1,), (1,))).astype(BF)
        dh = dot(cot[...], w2[0], ((1,), (1,)))
        dh_s[...] = dh + dot(adj[...], dagg, ((0,), (0,)))

    def features_out():
        wait_for(xv, loc_sem.at[0])

        @pl.loop(1, n)
        def _(k):
            p = lax.rem(me + k, n)
            remote(
                xv.at[p], mv.at[0, me], pair_sem.at[2], pair_sem.at[3], p,
            ).start()

        pltpu.make_async_copy(
            xv.at[me], mv.at[0, me], pair_sem.at[3]
        ).start()

    @pl.loop(1, n)
    def _(k):
        remote(colv, coli.at[me], pair_sem.at[0], pair_sem.at[1], lax.rem(me + k, n)).start()

    pltpu.make_async_copy(colv, coli.at[me], pair_sem.at[1]).start()

    def before_relay():
        features_out()
        backward_start()

    gather = Gather(pack, ag_send, ag_recv)
    gather.run(before_relay)
    wait_for(coli, pair_sem.at[1])
    to_smem = pltpu.make_async_copy(coli, cols_s, loc_sem.at[1])
    to_smem.start()
    to_smem.wait()

    def aggregate(r):
        total = jnp.zeros((sl, tile), F32)
        for s in range(slots):
            total += dot(xv[cols_s[r, 0, s]], pack[r, s * tile : (s + 1) * tile, :], ((1,), (1,)))
        agg[r] = total.astype(BF)

        @pl.when(r != me)
        def _():
            remote(agg.at[r], mv.at[1, me], pair_sem.at[4], pair_sem.at[5], r).start()

        @pl.when(r == me)
        def _():
            pltpu.make_async_copy(agg.at[r], mv.at[1, me], pair_sem.at[5]).start()

    half_n = n // 2

    @pl.loop(0, half_n)
    def _(j):
        aggregate(lax.rem(chip + j, half_n) * 2 + core)

    @pl.loop(0, half_n)
    def _(j):
        r = lax.rem(chip + j, half_n) * 2 + 1 - core
        gather.wait(0, r)
        gather.wait(1, r)
        aggregate(r)

    def project(k):
        at = trows + k * 2 * sl
        w = jnp.concatenate(
            [
                pack[:, at + h * sl : at + (h + 1) * sl, :].reshape(n * sl, half_w)
                for h in range(2)
            ],
            axis=1,
        )
        return dot(mv[k].reshape(n * sl, tile), w, ((0,), (0,)))

    wait_for(mv.at[0], pair_sem.at[3])
    acc[...] = project(0) + b1[...]
    wait_for(mv.at[1], pair_sem.at[5])
    z = acc[...] + project(1)
    sig = 1.0 / (1.0 + jnp.exp(-z))
    h_one = (z * sig).astype(BF)
    dz = (dh_s[...] * sig * (1.0 + z * (1.0 - sig))).astype(BF)
    dzb[me] = dz
    bs[0:1, :] = jnp.sum(dz.astype(F32), axis=0, keepdims=True)

    def forward():
        agg_two = dot(adj[...], h_one).astype(BF)
        g0 = dot(h_one, cot[...], ((0,), (0,)))
        g1 = dot(agg_two, cot[...], ((0,), (0,)))
        w2s[: n // 2] = g0.reshape(n // 2, rows, hid).astype(w2s.dtype)
        w2s[n // 2 :] = g1.reshape(n // 2, rows, hid).astype(w2s.dtype)

        @pl.loop(1, n)
        def _(k):
            p = lax.rem(me + k, n)
            remote(w2s.at[p], w2r.at[me], pair_sem.at[6], pair_sem.at[7], p).start()
            remote(bs, bb.at[me], pair_sem.at[8], pair_sem.at[9], p).start()

        pltpu.make_async_copy(w2s.at[me], w2r.at[me], pair_sem.at[7]).start()
        pltpu.make_async_copy(bs, bb.at[me], pair_sem.at[9]).start()
        z2 = dot(h_one, w2[0]) + dot(agg_two, w2[1]) + b2[...]
        out2[...] = z2.astype(BF)

    dgather = Gather(dzb, dz_send, dz_recv)
    dgather.run(forward)

    wait_for(w2r, pair_sem.at[7])
    wait_for(bb, pair_sem.at[9])
    dps[0:rows, :] = jnp.sum(w2r[...].astype(F32), axis=0)
    dps[rows:, :] = jnp.sum(bb[...], axis=0)

    def over_replicas(src, dst, ssem, rsem):
        @pl.loop(1, dp)
        def _(k):
            remote(src, dst.at[my_dp], ssem, rsem, lax.rem(my_dp + k, dp), "dp").start()

        pltpu.make_async_copy(src, dst.at[my_dp], rsem).start()

    over_replicas(dps, dpr, pair_sem.at[10], pair_sem.at[11])

    acc[...] = jnp.zeros_like(acc)

    def weight(r):
        lhs = jnp.concatenate([xv[r], agg[r]], axis=0)
        acc[0 : 2 * sl, :] += dot(lhs, dzb[r])

    @pl.loop(0, half_n)
    def _(j):
        weight(lax.rem(chip + j, half_n) * 2 + core)

    wait_for(dpr, pair_sem.at[11])
    total = dpr[0]
    for k in range(1, dp):
        total = total + dpr[k]
    g2s[...] = total[0:rows].astype(g2s.dtype)
    gb1[...] = total[rows : rows + 1]
    gb2[...] = total[rows + 1 : rows + 2]

    @pl.loop(1, n)
    def _(k):
        remote(g2s, g2r.at[me], pair_sem.at[12], pair_sem.at[13], lax.rem(me + k, n)).start()

    pltpu.make_async_copy(g2s, g2r.at[me], pair_sem.at[13]).start()

    @pl.loop(0, half_n)
    def _(j):
        r = lax.rem(chip + j, half_n) * 2 + 1 - core
        dgather.wait(0, r)
        dgather.wait(1, r)
        weight(r)

    w1s[...] = acc[0 : 2 * sl, :].astype(w1s.dtype)
    over_replicas(w1s, w1r, pair_sem.at[14], pair_sem.at[15])
    gather.finish()
    dgather.finish()

    def sent(ref, sem):
        wait_for(ref, sem)

    sent(coli.at[pl.ds(0, n - 1)], pair_sem.at[0])
    sent(mv.at[0, pl.ds(0, n - 1)], pair_sem.at[2])
    sent(mv.at[1, pl.ds(0, n - 1)], pair_sem.at[4])
    sent(w2r.at[pl.ds(0, n - 1)], pair_sem.at[6])
    sent(bb.at[pl.ds(0, n - 1)], pair_sem.at[8])
    wait_for(g2r, pair_sem.at[13])
    gw2[...] = g2r[...].astype(F32).reshape(n * rows, hid)
    sent(g2r.at[pl.ds(0, n - 1)], pair_sem.at[12])
    if dp > 1:
        sent(dpr.at[pl.ds(0, dp - 1)], pair_sem.at[10])
    wait_for(w1r, pair_sem.at[15])
    total = w1r[0].astype(F32)
    for k in range(1, dp):
        total = total + w1r[k].astype(F32)
    gw1[...] = total
    if dp > 1:
        sent(w1r.at[pl.ds(0, dp - 1)], pair_sem.at[14])


def local(n, dp, x_feat, tiles_one, tile_cols, tile_counts, w_one, b_one, adj_two, w_two, b_two, cotangent):
    zs, xs = grid_of(n)
    sl, width = x_feat.shape[1:]
    tile = adj_two.shape[-1]
    slots = tiles_one.shape[1]
    hid = w_one.shape[2]
    rows = 2 * hid // n
    narrow = BF if rows % 16 == 0 else F32
    packed = slots * tile + 4 * sl
    vmem = pl.BlockSpec(memory_space=pltpu.VMEM)
    dma = pltpu.SemaphoreType.DMA
    out2, gw1, gb1, gw2, gb2 = pl.pallas_call(
        functools.partial(kernel, n, dp, zs, xs),
        out_shape=(
            jax.ShapeDtypeStruct((tile, hid), BF),
            jax.ShapeDtypeStruct((2 * sl, hid), F32),
            jax.ShapeDtypeStruct((1, hid), F32),
            jax.ShapeDtypeStruct((2 * hid, hid), F32),
            jax.ShapeDtypeStruct((1, hid), F32),
        ),
        in_specs=[pl.BlockSpec(memory_space=pltpu.HBM)] * 10,
        out_specs=(vmem,) * 5,
        scratch_shapes=[
            pltpu.VMEM((width // tile, sl, tile), BF),
            pltpu.VMEM((n, packed, tile), BF),
            pltpu.VMEM((2, n, sl, tile), BF),
            pltpu.VMEM((n, sl, tile), BF),
            pltpu.VMEM((n, tile, hid), BF),
            pltpu.VMEM((1, 128), jnp.int32),
            pltpu.VMEM((n, 1, 128), jnp.int32),
            pltpu.SMEM((n, 1, 128), jnp.int32),
            pltpu.VMEM((tile, hid), F32),
            pltpu.VMEM((max(tile, 2 * sl), hid), F32),
            pltpu.VMEM((n, rows, hid), narrow),
            pltpu.VMEM((n, rows, hid), narrow),
            pltpu.VMEM((rows, hid), narrow),
            pltpu.VMEM((n, rows, hid), narrow),
            pltpu.VMEM((8, hid), F32),
            pltpu.VMEM((n, 8, hid), F32),
            pltpu.VMEM((rows + 8, hid), F32),
            pltpu.VMEM((dp, rows + 8, hid), F32),
            pltpu.VMEM((2 * sl, hid), BF),
            pltpu.VMEM((dp, 2 * sl, hid), BF),
            pltpu.VMEM((slots, tile, tile), BF),
            pltpu.SMEM((1, slots), jnp.int32),
            pltpu.SMEM((1, 1), jnp.int32),
            pltpu.VMEM((2, sl, hid), BF),
            pltpu.VMEM((1, hid), F32),
            pltpu.VMEM((tile, tile), BF),
            pltpu.VMEM((2, hid, hid), BF),
            pltpu.VMEM((1, hid), F32),
            pltpu.VMEM((tile, hid), BF),
            dma((2, n, xs + 2)),
            dma((2, n)),
            dma((2, n, xs + 2)),
            dma((2, n)),
            dma((16,)),
            dma((11,)),
        ],
        compiler_params=pltpu.CompilerParams(
            collective_id=0, has_side_effects=True, vmem_limit_bytes=63 * 1024 * 1024
        ),
    )(
        x_feat[0], tiles_one[0], tile_cols, tile_counts, w_one, b_one[None], adj_two[0], w_two,
        b_two[None], cotangent[0],
    )
    return (
        out2[None], gw1.reshape(2, sl, hid), gb1[0], gw2.reshape(2, hid, hid), gb2[0],
    )


def solution(mesh):
    in_specs = (
        P("dp", "feat", None),
        P("dp", "feat", None, None),
        P("dp", "feat"),
        P("dp", "feat"),
        P(None, "feat", None),
        P(),
        P("dp", "feat", None),
        P(),
        P(),
        P("dp", "feat", None),
    )
    out_specs = (P("dp", "feat", None), P(None, "feat", None), P(), P(), P())
    return jax.shard_map(
        functools.partial(local, mesh.shape["feat"], mesh.shape["dp"]),
        mesh=mesh, in_specs=in_specs, out_specs=out_specs, check_vma=False,
    )
```

```python
import functools
import math

import jax
import jax.numpy as jnp
from jax import lax
from jax.experimental import pallas as pl
from jax.experimental.pallas import tpu as pltpu
from jax.sharding import PartitionSpec as P

BF = jnp.bfloat16
F32 = jnp.float32


def dot(a, b, dims=((1,), (0,))):
    return lax.dot_general(a, b, (dims, ((), ())), preferred_element_type=F32)


def grid_of(n):
    x = max(math.isqrt(n // 4), 1)
    while (n // 2) % x:
        x -= 1
    return n // 2 // x, x


def kernel(
    n, dp, zs, xs,
    x_hbm, tiles_h, cols_h, counts_h, w1_h, b1_h, adj_h, w2_h, b2_h, cot_h,
    out2, gw1, gb1, gw2, gb2,
    xv, pack, mv, agg, dzb, colv, coli, cols_s, dh_s, acc,
    w2s, w2x, w2u, w2r, g2s, g2r, bs, bb, bt, br, dps, dpr, w1s, w1r,
    tiles, cols, counts, w1, b1, adj, w2, b2, cot,
    ag_send, ag_recv, dz_send, dz_recv, pair_sem, loc_sem,
):
    me = lax.axis_index("feat")
    my_dp = lax.axis_index("dp")
    core = lax.rem(me, 2)
    chip = lax.div(me, 2)
    xx = lax.rem(chip, xs)
    zz = lax.div(chip, xs)
    sl = w1.shape[1]
    tile = adj.shape[0]
    slots = tiles.shape[0]
    trows = slots * tile
    hid = w1.shape[2]
    half_w = hid // 2
    rows = w2s.shape[2]
    half_n = n // 2

    def index(z, x, c):
        return (z * xs + x) * 2 + c

    def remote(src, dst, ssem, rsem, peer, axis="feat"):
        return pltpu.make_async_remote_copy(
            src_ref=src, dst_ref=dst, send_sem=ssem, recv_sem=rsem,
            device_id={axis: peer}, device_id_type=pl.DeviceIdType.MESH,
        )

    def wait_for(ref, sem):
        pltpu.make_async_copy(ref, ref, sem).wait()

    early = [
        pltpu.make_async_copy(src, dst, loc_sem.at[2 + k])
        for k, (src, dst) in enumerate(
            [
                (cols_h, cols), (counts_h, counts), (tiles_h, tiles), (w1_h, w1), (cot_h, cot),
                (w2_h, w2), (adj_h, adj), (b1_h, b1), (b2_h, b2),
            ]
        )
    ]
    for copy in early:
        copy.start()
    barrier = pltpu.get_barrier_semaphore()

    @pl.loop(1, n)
    def _(k):
        pl.semaphore_signal(
            barrier, inc=1, device_id={"feat": lax.rem(me + k, n)}, device_id_type=pl.DeviceIdType.MESH
        )

    @pl.loop(1, dp)
    def _(k):
        pl.semaphore_signal(
            barrier, inc=1, device_id={"dp": lax.rem(my_dp + k, dp)}, device_id_type=pl.DeviceIdType.MESH
        )

    @pl.loop(0, xv.shape[0])
    def _(b):
        at = pl.multiple_of(b * tile, tile)
        pltpu.make_async_copy(x_hbm.at[:, pl.ds(at, tile)], xv.at[b], loc_sem.at[0]).start()

    for copy in early:
        copy.wait()
    count = counts[0, 0]
    lane = lax.broadcasted_iota(jnp.int32, (1, 128), 1)
    info = jnp.zeros((1, 128), jnp.int32)
    for s in range(slots):
        live = jnp.minimum(jnp.maximum(count - s, 0), 1).astype(F32)
        pack[me, s * tile : (s + 1) * tile, :] = (tiles[s].astype(F32) * live).astype(BF)
        info = jnp.where(lane == s, cols[0, s], info)
    colv[...] = info
    for k in range(2):
        for h in range(2):
            at = trows + (k * 2 + h) * sl
            pack[me, at : at + sl, :] = w1[k, :, h * half_w : (h + 1) * half_w]
    bs[:, hid:] = jnp.sum(cot[...].astype(F32), axis=0, keepdims=True)
    dagg = dot(cot[...], w2[1], ((1,), (1,))).astype(BF)
    dh = dot(cot[...], w2[0], ((1,), (1,)))
    dh_s[...] = dh + dot(adj[...], dagg, ((0,), (0,)))
    pl.semaphore_wait(barrier, n - 1 + dp - 1)

    class Gather:
        def __init__(self, buf, send, recv):
            self.buf, self.send, self.recv = buf, send, recv
            self.half = buf.shape[1] // 2

        def view(self, h, src):
            return self.buf.at[src, pl.ds(h * self.half, self.half), :]

        def copy(self, h, src, slot, peer):
            v = self.view(h, src)
            return remote(v, v, self.send.at[h, src, slot], self.recv.at[h, src], peer)

        def wait(self, h, src):
            wait_for(self.view(h, src), self.recv.at[h, src])

        def up(self, h, src, act):
            @pl.when(zz < zs - 1)
            def _():
                act(self.copy(h, src, 0, index(zz + 1, xx, core)))

        def down(self, h, src, act):
            @pl.when(zz > 0)
            def _():
                act(self.copy(h, src, 1, index(zz - 1, xx, core)))

        def across(self, h, src, act):
            for k in range(1, xs):
                act(self.copy(h, src, 1 + k, index(zz, lax.rem(xx + k, xs), core)))

        def sibling(self, h, src, act):
            act(self.copy(h, src, xs + 1, index(zz, xx, 1 - core)))

        def walk(self, act, first, arrive, ready):
            def from_sibling(z, x):
                src = index(z, x, 1 - core)
                arrive(0, src)
                arrive(1, src)
                ready(src)

            for h in (1, 0):
                self.across(h, me, act)
                self.up(h, me, act)
                self.down(h, me, act)
                self.sibling(h, me, act)
            first()
            for k in range(1, xs):
                src = index(zz, lax.rem(xx + k, xs), core)
                arrive(1, src)
                self.up(1, src, act)
                self.down(1, src, act)
                self.sibling(1, src, act)
            ready(me)

            @pl.loop(1, zs)
            def _(k):
                @pl.when(zz - k >= 0)
                def _():
                    src = index(zz - k, xx, core)
                    arrive(0, src)
                    self.up(0, src, act)
                    self.across(0, src, act)
                    self.sibling(0, src, act)

                @pl.when(zz + k < zs)
                def _():
                    src = index(zz + k, xx, core)
                    arrive(0, src)
                    self.down(0, src, act)
                    self.across(0, src, act)
                    self.sibling(0, src, act)

                for j in range(xs):
                    other = lax.rem(xx + j, xs)

                    @pl.when(zz - k >= 0)
                    def _():
                        src = index(zz - k, other, core)
                        arrive(1, src)
                        self.up(1, src, act)
                        self.sibling(1, src, act)

                    @pl.when(zz + k < zs)
                    def _():
                        src = index(zz + k, other, core)
                        arrive(1, src)
                        self.down(1, src, act)
                        self.sibling(1, src, act)

                @pl.when(zz - k >= 0)
                def _():
                    ready(index(zz - k, xx, core))

                @pl.when(zz + k < zs)
                def _():
                    ready(index(zz + k, xx, core))

                @pl.when(zz - k + 1 >= 0)
                def _():
                    from_sibling(zz - k + 1, xx)

                @pl.when((zz + k - 1 < zs) & (k > 1))
                def _():
                    from_sibling(zz + k - 1, xx)

            @pl.loop(0, zs)
            def _(k):
                z = lax.rem(zz + k, zs)
                for j in range(1, xs):
                    src = index(z, lax.rem(xx + j, xs), core)
                    arrive(0, src)
                    self.sibling(0, src, act)
                    ready(src)

            for z in ((zz - zs + 1), (zz + zs - 1)):
                @pl.when((z >= 0) & (z < zs))
                def _():
                    from_sibling(z, xx)

            @pl.loop(0, zs)
            def _(k):
                z = lax.rem(zz + k, zs)
                for j in range(1, xs):
                    from_sibling(z, lax.rem(xx + j, xs))

        def run(self, first, ready):
            self.walk(lambda c: c.start(), first, self.wait, ready)

        def finish(self):
            self.walk(lambda c: c.wait_send(), lambda: None, lambda h, s: None, lambda s: None)

    def features_out():
        @pl.loop(1, n)
        def _(k):
            p = lax.rem(me + k, n)
            remote(
                x_hbm.at[:, pl.ds(pl.multiple_of(p * tile, tile), tile)], mv.at[0, me],
                pair_sem.at[2], pair_sem.at[3], p,
            ).start()

        at = pl.multiple_of(me * tile, tile)
        pltpu.make_async_copy(x_hbm.at[:, pl.ds(at, tile)], mv.at[0, me], pair_sem.at[3]).start()

    @pl.loop(1, n)
    def _(k):
        remote(colv, coli.at[me], pair_sem.at[0], pair_sem.at[1], lax.rem(me + k, n)).start()

    pltpu.make_async_copy(colv, coli.at[me], pair_sem.at[1]).start()

    def before_relay():
        features_out()
        wait_for(coli, pair_sem.at[1])
        to_smem = pltpu.make_async_copy(coli, cols_s, loc_sem.at[1])
        to_smem.start()
        to_smem.wait()
        wait_for(xv, loc_sem.at[0])

    gather = Gather(pack, ag_send, ag_recv)

    def aggregate(r):
        total = jnp.zeros((sl, tile), F32)
        for s in range(slots):
            total += dot(xv[cols_s[r, 0, s]], pack[r, s * tile : (s + 1) * tile, :], ((1,), (1,)))
        agg[r] = total.astype(BF)

        @pl.when(r != me)
        def _():
            remote(agg.at[r], mv.at[1, me], pair_sem.at[4], pair_sem.at[5], r).start()

        @pl.when(r == me)
        def _():
            pltpu.make_async_copy(agg.at[r], mv.at[1, me], pair_sem.at[5]).start()

    gather.run(before_relay, aggregate)

    def project(k):
        at = trows + k * 2 * sl
        w = jnp.concatenate(
            [
                pack[:, at + h * sl : at + (h + 1) * sl, :].reshape(n * sl, half_w)
                for h in range(2)
            ],
            axis=1,
        )
        return dot(mv[k].reshape(n * sl, tile), w, ((0,), (0,)))

    wait_for(mv.at[0], pair_sem.at[3])
    acc[...] = project(0) + b1[...]
    wait_for(mv.at[1], pair_sem.at[5])
    z = acc[...] + project(1)
    sig = 1.0 / (1.0 + jnp.exp(-z))
    h_one = (z * sig).astype(BF)
    dz = (dh_s[...] * sig * (1.0 + z * (1.0 - sig))).astype(BF)
    dzb[me] = dz
    bs[:, :hid] = jnp.sum(dz.astype(F32), axis=0, keepdims=True)

    def forward():
        agg_two = dot(adj[...], h_one).astype(BF)
        g0 = dot(h_one, cot[...], ((0,), (0,)))
        g1 = dot(agg_two, cot[...], ((0,), (0,)))
        for j in range(n):
            g = (g0, g1)[j // half_n]
            at = (j % half_n) * rows
            w2s[j % 2, j // 2] = g[at : at + rows].astype(w2s.dtype)
        remote(w2s.at[1 - core], w2x, pair_sem.at[6], pair_sem.at[7], index(zz, xx, 1 - core)).start()

        @pl.loop(1, n)
        def _(k):
            remote(bs, bb.at[me], pair_sem.at[8], pair_sem.at[9], lax.rem(me + k, n)).start()

        pltpu.make_async_copy(bs, bb.at[me], pair_sem.at[9]).start()
        z2 = dot(h_one, w2[0]) + dot(agg_two, w2[1]) + b2[...]
        out2[...] = z2.astype(BF)
        wait_for(w2x, pair_sem.at[7])
        w2u[...] = (w2s[core].astype(F32) + w2x[...].astype(F32)).astype(w2u.dtype)

        @pl.loop(1, half_n)
        def _(k):
            p = lax.rem(chip + k, half_n)
            remote(w2u.at[p], w2r.at[chip], pair_sem.at[10], pair_sem.at[11], p * 2 + core).start()

        pltpu.make_async_copy(w2u.at[chip], w2r.at[chip], pair_sem.at[11]).start()

    acc[...] = jnp.zeros_like(acc)

    def weight(r):
        lhs = jnp.concatenate([xv[r], agg[r]], axis=0)
        acc[0 : 2 * sl, :] += dot(lhs, dzb[r])

    def over_replicas(src, dst, ssem, rsem):
        @pl.loop(1, dp)
        def _(k):
            remote(src, dst.at[my_dp], ssem, rsem, lax.rem(my_dp + k, dp), "dp").start()

        pltpu.make_async_copy(src, dst.at[my_dp], rsem).start()

    dgather = Gather(dzb, dz_send, dz_recv)
    dgather.run(forward, weight)
    w1s[...] = acc[0 : 2 * sl, :].astype(w1s.dtype)
    over_replicas(w1s, w1r, pair_sem.at[14], pair_sem.at[15])

    wait_for(w2r, pair_sem.at[11])
    dps[...] = jnp.sum(w2r[...].astype(F32), axis=0)
    over_replicas(dps, dpr, pair_sem.at[12], pair_sem.at[13])
    wait_for(bb, pair_sem.at[9])
    bt[...] = jnp.sum(bb[...], axis=0)
    over_replicas(bt, br, pair_sem.at[16], pair_sem.at[17])
    wait_for(dpr, pair_sem.at[13])
    total = dpr[0]
    for k in range(1, dp):
        total = total + dpr[k]
    g2s[...] = total.astype(g2s.dtype)

    @pl.loop(1, half_n)
    def _(k):
        p = lax.rem(chip + k, half_n) * 2 + core
        remote(g2s, g2r.at[core, chip], pair_sem.at[18], pair_sem.at[19], p).start()

    pltpu.make_async_copy(g2s, g2r.at[core, chip], pair_sem.at[19]).start()
    gather.finish()
    dgather.finish()
    wait_for(coli.at[pl.ds(0, n - 1)], pair_sem.at[0])
    wait_for(mv.at[0, pl.ds(0, n - 1)], pair_sem.at[2])
    wait_for(mv.at[1, pl.ds(0, n - 1)], pair_sem.at[4])
    wait_for(w2x, pair_sem.at[6])
    wait_for(bb.at[pl.ds(0, n - 1)], pair_sem.at[8])
    wait_for(w2r.at[pl.ds(0, half_n - 1)], pair_sem.at[10])
    wait_for(br, pair_sem.at[17])
    bias = br[0]
    for k in range(1, dp):
        bias = bias + br[k]
    gb1[...] = bias[:, :hid]
    gb2[...] = bias[:, hid:]
    wait_for(w1r, pair_sem.at[15])
    total = w1r[0].astype(F32)
    for k in range(1, dp):
        total = total + w1r[k].astype(F32)
    gw1[...] = total
    wait_for(g2r.at[core], pair_sem.at[19])
    last = remote(
        g2r.at[core], g2r.at[core], pair_sem.at[20], pair_sem.at[21], index(zz, xx, 1 - core)
    )
    last.start()
    wait_for(g2r.at[1 - core], pair_sem.at[21])
    for j in range(n):
        gw2[j * rows : (j + 1) * rows] = g2r[j % 2, j // 2].astype(F32)
    last.wait_send()
    wait_for(g2r.at[0, pl.ds(0, half_n - 1)], pair_sem.at[18])
    if dp > 1:
        wait_for(dpr.at[pl.ds(0, dp - 1)], pair_sem.at[12])
        wait_for(w1r.at[pl.ds(0, dp - 1)], pair_sem.at[14])
        wait_for(br.at[pl.ds(0, dp - 1)], pair_sem.at[16])


def local(n, dp, x_feat, tiles_one, tile_cols, tile_counts, w_one, b_one, adj_two, w_two, b_two, cotangent):
    zs, xs = grid_of(n)
    sl, width = x_feat.shape[1:]
    tile = adj_two.shape[-1]
    slots = tiles_one.shape[1]
    hid = w_one.shape[2]
    rows = 2 * hid // n
    narrow = BF if rows % 16 == 0 else F32
    packed = slots * tile + 4 * sl
    vmem = pl.BlockSpec(memory_space=pltpu.VMEM)
    dma = pltpu.SemaphoreType.DMA
    out2, gw1, gb1, gw2, gb2 = pl.pallas_call(
        functools.partial(kernel, n, dp, zs, xs),
        out_shape=(
            jax.ShapeDtypeStruct((tile, hid), BF),
            jax.ShapeDtypeStruct((2 * sl, hid), F32),
            jax.ShapeDtypeStruct((1, hid), F32),
            jax.ShapeDtypeStruct((2 * hid, hid), F32),
            jax.ShapeDtypeStruct((1, hid), F32),
        ),
        in_specs=[pl.BlockSpec(memory_space=pltpu.HBM)] * 10,
        out_specs=(vmem,) * 5,
        scratch_shapes=[
            pltpu.VMEM((width // tile, sl, tile), BF),
            pltpu.VMEM((n, packed, tile), BF),
            pltpu.VMEM((2, n, sl, tile), BF),
            pltpu.VMEM((n, sl, tile), BF),
            pltpu.VMEM((n, tile, hid), BF),
            pltpu.VMEM((1, 128), jnp.int32),
            pltpu.VMEM((n, 1, 128), jnp.int32),
            pltpu.SMEM((n, 1, 128), jnp.int32),
            pltpu.VMEM((tile, hid), F32),
            pltpu.VMEM((max(tile, 2 * sl), hid), F32),
            pltpu.VMEM((2, n // 2, rows, hid), narrow),
            pltpu.VMEM((n // 2, rows, hid), narrow),
            pltpu.VMEM((n // 2, rows, hid), narrow),
            pltpu.VMEM((n // 2, rows, hid), narrow),
            pltpu.VMEM((rows, hid), narrow),
            pltpu.VMEM((2, n // 2, rows, hid), narrow),
            pltpu.VMEM((1, 2 * hid), F32),
            pltpu.VMEM((n, 1, 2 * hid), F32),
            pltpu.VMEM((1, 2 * hid), F32),
            pltpu.VMEM((dp, 1, 2 * hid), F32),
            pltpu.VMEM((rows, hid), F32),
            pltpu.VMEM((dp, rows, hid), F32),
            pltpu.VMEM((2 * sl, hid), BF),
            pltpu.VMEM((dp, 2 * sl, hid), BF),
            pltpu.VMEM((slots, tile, tile), BF),
            pltpu.SMEM((1, slots), jnp.int32),
            pltpu.SMEM((1, 1), jnp.int32),
            pltpu.VMEM((2, sl, hid), BF),
            pltpu.VMEM((1, hid), F32),
            pltpu.VMEM((tile, tile), BF),
            pltpu.VMEM((2, hid, hid), BF),
            pltpu.VMEM((1, hid), F32),
            pltpu.VMEM((tile, hid), BF),
            dma((2, n, xs + 2)),
            dma((2, n)),
            dma((2, n, xs + 2)),
            dma((2, n)),
            dma((22,)),
            dma((11,)),
        ],
        compiler_params=pltpu.CompilerParams(
            collective_id=0, has_side_effects=True, vmem_limit_bytes=63 * 1024 * 1024
        ),
    )(
        x_feat[0], tiles_one[0], tile_cols, tile_counts, w_one, b_one[None], adj_two[0], w_two,
        b_two[None], cotangent[0],
    )
    return (
        out2[None], gw1.reshape(2, sl, hid), gb1[0], gw2.reshape(2, hid, hid), gb2[0],
    )


def solution(mesh):
    in_specs = (
        P("dp", "feat", None),
        P("dp", "feat", None, None),
        P("dp", "feat"),
        P("dp", "feat"),
        P(None, "feat", None),
        P(),
        P("dp", "feat", None),
        P(),
        P(),
        P("dp", "feat", None),
    )
    out_specs = (P("dp", "feat", None), P(None, "feat", None), P(), P(), P())
    return jax.shard_map(
        functools.partial(local, mesh.shape["feat"], mesh.shape["dp"]),
        mesh=mesh, in_specs=in_specs, out_specs=out_specs, check_vma=False,
    )
```

```python
import functools
import math

import jax
import jax.numpy as jnp
from jax import lax
from jax.experimental import pallas as pl
from jax.experimental.pallas import tpu as pltpu
from jax.sharding import PartitionSpec as P

BF = jnp.bfloat16
F32 = jnp.float32


def dot(a, b, dims=((1,), (0,))):
    return lax.dot_general(a, b, (dims, ((), ())), preferred_element_type=F32)


def grid_of(n):
    x = max(math.isqrt(n // 4), 1)
    while (n // 2) % x:
        x -= 1
    return n // 2 // x, x


def kernel(
    n, dp, zs, xs,
    x_hbm, tiles_h, cols_h, counts_h, w1_h, b1_h, adj_h, w2_h, b2_h, cot_h,
    out2, gw1, gb1, gw2, gb2,
    xv, pack, mv, agg, dzb, colv, coli, cols_s, dh_s, acc,
    w2s, w2x, w2u, w2r, g2s, g2r, bs, bb, bt, br, dps, dpr, w1s, w1r,
    tiles, cols, counts, w1, b1, adj, w2, b2, cot,
    ag_send, ag_recv, dz_send, dz_recv, pair_sem, loc_sem,
):
    me = lax.axis_index("feat")
    my_dp = lax.axis_index("dp")
    core = lax.rem(me, 2)
    chip = lax.div(me, 2)
    xx = lax.rem(chip, xs)
    zz = lax.div(chip, xs)
    sl = w1.shape[1]
    tile = adj.shape[0]
    slots = tiles.shape[0]
    trows = slots * tile
    hid = w1.shape[2]
    half_w = hid // 2
    rows = w2s.shape[2]
    half_n = n // 2

    def index(z, x, c):
        return (z * xs + x) * 2 + c

    def remote(src, dst, ssem, rsem, peer, axis="feat"):
        return pltpu.make_async_remote_copy(
            src_ref=src, dst_ref=dst, send_sem=ssem, recv_sem=rsem,
            device_id={axis: peer}, device_id_type=pl.DeviceIdType.MESH,
        )

    def wait_for(ref, sem):
        pltpu.make_async_copy(ref, ref, sem).wait()

    early = [
        pltpu.make_async_copy(src, dst, loc_sem.at[2 + k])
        for k, (src, dst) in enumerate(
            [
                (cols_h, cols), (counts_h, counts), (tiles_h, tiles), (w1_h, w1), (cot_h, cot),
                (w2_h, w2), (adj_h, adj), (b1_h, b1), (b2_h, b2),
            ]
        )
    ]
    for copy in early:
        copy.start()
    barrier = pltpu.get_barrier_semaphore()

    @pl.loop(1, n)
    def _(k):
        pl.semaphore_signal(
            barrier, inc=1, device_id={"feat": lax.rem(me + k, n)}, device_id_type=pl.DeviceIdType.MESH
        )

    @pl.loop(1, dp)
    def _(k):
        pl.semaphore_signal(
            barrier, inc=1, device_id={"dp": lax.rem(my_dp + k, dp)}, device_id_type=pl.DeviceIdType.MESH
        )

    @pl.loop(0, xv.shape[0])
    def _(b):
        at = pl.multiple_of(b * tile, tile)
        pltpu.make_async_copy(x_hbm.at[:, pl.ds(at, tile)], xv.at[b], loc_sem.at[0]).start()

    for copy in early:
        copy.wait()
    count = counts[0, 0]
    lane = lax.broadcasted_iota(jnp.int32, (1, 128), 1)
    info = jnp.zeros((1, 128), jnp.int32)
    for s in range(slots):
        live = jnp.minimum(jnp.maximum(count - s, 0), 1).astype(F32)
        pack[me, s * tile : (s + 1) * tile, :] = (tiles[s].astype(F32) * live).astype(BF)
        info = jnp.where(lane == s, cols[0, s], info)
    colv[...] = info
    for k in range(2):
        for h in range(2):
            at = trows + (k * 2 + h) * sl
            pack[me, at : at + sl, :] = w1[k, :, h * half_w : (h + 1) * half_w]
    pl.semaphore_wait(barrier, n - 1 + dp - 1)

    class Gather:
        def __init__(self, buf, send, recv):
            self.buf, self.send, self.recv = buf, send, recv
            self.half = buf.shape[1] // 2

        def view(self, h, src):
            return self.buf.at[src, pl.ds(h * self.half, self.half), :]

        def copy(self, h, src, slot, peer):
            v = self.view(h, src)
            return remote(v, v, self.send.at[h, src, slot], self.recv.at[h, src], peer)

        def wait(self, h, src):
            wait_for(self.view(h, src), self.recv.at[h, src])

        def up(self, h, src, act):
            @pl.when(zz < zs - 1)
            def _():
                act(self.copy(h, src, 0, index(zz + 1, xx, core)))

        def down(self, h, src, act):
            @pl.when(zz > 0)
            def _():
                act(self.copy(h, src, 1, index(zz - 1, xx, core)))

        def across(self, h, src, act):
            for k in range(1, xs):
                act(self.copy(h, src, 1 + k, index(zz, lax.rem(xx + k, xs), core)))

        def sibling(self, h, src, act):
            act(self.copy(h, src, xs + 1, index(zz, xx, 1 - core)))

        def walk(self, act, first, arrive, ready, middle=lambda: None, late=lambda: None):
            def from_sibling(z, x):
                src = index(z, x, 1 - core)
                arrive(0, src)
                arrive(1, src)
                ready(src)

            for h in (1, 0):
                self.across(h, me, act)
                self.up(h, me, act)
                self.down(h, me, act)
                self.sibling(h, me, act)
            first()
            for k in range(1, xs):
                src = index(zz, lax.rem(xx + k, xs), core)
                arrive(1, src)
                self.up(1, src, act)
                self.down(1, src, act)
                self.sibling(1, src, act)
            ready(me)

            @pl.loop(1, zs)
            def _(k):
                @pl.when(zz - k >= 0)
                def _():
                    src = index(zz - k, xx, core)
                    arrive(0, src)
                    self.up(0, src, act)
                    self.across(0, src, act)
                    self.sibling(0, src, act)

                @pl.when(zz + k < zs)
                def _():
                    src = index(zz + k, xx, core)
                    arrive(0, src)
                    self.down(0, src, act)
                    self.across(0, src, act)
                    self.sibling(0, src, act)

                for j in range(xs):
                    other = lax.rem(xx + j, xs)

                    @pl.when(zz - k >= 0)
                    def _():
                        src = index(zz - k, other, core)
                        arrive(1, src)
                        self.up(1, src, act)
                        self.sibling(1, src, act)

                    @pl.when(zz + k < zs)
                    def _():
                        src = index(zz + k, other, core)
                        arrive(1, src)
                        self.down(1, src, act)
                        self.sibling(1, src, act)

                @pl.when(zz - k >= 0)
                def _():
                    ready(index(zz - k, xx, core))

                @pl.when(zz + k < zs)
                def _():
                    ready(index(zz + k, xx, core))

                @pl.when(zz - k + 1 >= 0)
                def _():
                    from_sibling(zz - k + 1, xx)

                @pl.when((zz + k - 1 < zs) & (k > 1))
                def _():
                    from_sibling(zz + k - 1, xx)

            middle()

            @pl.loop(0, zs)
            def _(k):
                z = lax.rem(zz + k, zs)
                for j in range(1, xs):
                    src = index(z, lax.rem(xx + j, xs), core)
                    arrive(0, src)
                    self.sibling(0, src, act)
                    ready(src)

            late()
            for z in ((zz - zs + 1), (zz + zs - 1)):
                @pl.when((z >= 0) & (z < zs))
                def _():
                    from_sibling(z, xx)

            @pl.loop(0, zs)
            def _(k):
                z = lax.rem(zz + k, zs)
                for j in range(1, xs):
                    from_sibling(z, lax.rem(xx + j, xs))

        def run(self, first, ready, *between):
            self.walk(lambda c: c.start(), first, self.wait, ready, *between)

        def finish(self):
            self.walk(lambda c: c.wait_send(), lambda: None, lambda h, s: None, lambda s: None)

    def features_out():
        @pl.loop(1, n)
        def _(k):
            p = lax.rem(me + k, n)
            remote(
                x_hbm.at[:, pl.ds(pl.multiple_of(p * tile, tile), tile)], mv.at[0, me],
                pair_sem.at[2], pair_sem.at[3], p,
            ).start()

        at = pl.multiple_of(me * tile, tile)
        pltpu.make_async_copy(x_hbm.at[:, pl.ds(at, tile)], mv.at[0, me], pair_sem.at[3]).start()

    @pl.loop(1, n)
    def _(k):
        remote(colv, coli.at[me], pair_sem.at[0], pair_sem.at[1], lax.rem(me + k, n)).start()

    pltpu.make_async_copy(colv, coli.at[me], pair_sem.at[1]).start()

    def before_relay():
        features_out()
        bs[:, hid:] = jnp.sum(cot[...].astype(F32), axis=0, keepdims=True)
        dagg = dot(cot[...], w2[1], ((1,), (1,))).astype(BF)
        dh = dot(cot[...], w2[0], ((1,), (1,)))
        dh_s[...] = dh + dot(adj[...], dagg, ((0,), (0,)))
        wait_for(coli, pair_sem.at[1])
        to_smem = pltpu.make_async_copy(coli, cols_s, loc_sem.at[1])
        to_smem.start()
        to_smem.wait()
        wait_for(xv, loc_sem.at[0])

    gather = Gather(pack, ag_send, ag_recv)

    def aggregate(r):
        total = jnp.zeros((sl, tile), F32)
        for s in range(slots):
            total += dot(xv[cols_s[r, 0, s]], pack[r, s * tile : (s + 1) * tile, :], ((1,), (1,)))
        agg[r] = total.astype(BF)

        @pl.when(r != me)
        def _():
            remote(agg.at[r], mv.at[1, me], pair_sem.at[4], pair_sem.at[5], r).start()

        @pl.when(r == me)
        def _():
            pltpu.make_async_copy(agg.at[r], mv.at[1, me], pair_sem.at[5]).start()

    gather.run(before_relay, aggregate)

    def project(k):
        at = trows + k * 2 * sl
        w = jnp.concatenate(
            [
                pack[:, at + h * sl : at + (h + 1) * sl, :].reshape(n * sl, half_w)
                for h in range(2)
            ],
            axis=1,
        )
        return dot(mv[k].reshape(n * sl, tile), w, ((0,), (0,)))

    wait_for(mv.at[0], pair_sem.at[3])
    acc[...] = project(0) + b1[...]
    wait_for(mv.at[1], pair_sem.at[5])
    z = acc[...] + project(1)
    sig = 1.0 / (1.0 + jnp.exp(-z))
    h_one = (z * sig).astype(BF)
    dz = (dh_s[...] * sig * (1.0 + z * (1.0 - sig))).astype(BF)
    dzb[me] = dz
    bs[:, :hid] = jnp.sum(dz.astype(F32), axis=0, keepdims=True)

    def forward():
        agg_two = dot(adj[...], h_one).astype(BF)
        g0 = dot(h_one, cot[...], ((0,), (0,)))
        g1 = dot(agg_two, cot[...], ((0,), (0,)))
        for j in range(n):
            g = (g0, g1)[j // half_n]
            at = (j % half_n) * rows
            w2s[j % 2, j // 2] = g[at : at + rows].astype(w2s.dtype)
        remote(w2s.at[1 - core], w2x, pair_sem.at[6], pair_sem.at[7], index(zz, xx, 1 - core)).start()

        @pl.loop(1, n)
        def _(k):
            remote(bs, bb.at[me], pair_sem.at[8], pair_sem.at[9], lax.rem(me + k, n)).start()

        pltpu.make_async_copy(bs, bb.at[me], pair_sem.at[9]).start()
        z2 = dot(h_one, w2[0]) + dot(agg_two, w2[1]) + b2[...]
        out2[...] = z2.astype(BF)
        wait_for(w2x, pair_sem.at[7])
        w2u[...] = (w2s[core].astype(F32) + w2x[...].astype(F32)).astype(w2u.dtype)

        @pl.loop(1, half_n)
        def _(k):
            p = lax.rem(chip + k, half_n)
            remote(w2u.at[p], w2r.at[chip], pair_sem.at[10], pair_sem.at[11], p * 2 + core).start()

        pltpu.make_async_copy(w2u.at[chip], w2r.at[chip], pair_sem.at[11]).start()

    acc[...] = jnp.zeros_like(acc)

    def weight(r):
        lhs = jnp.concatenate([xv[r], agg[r]], axis=0)
        acc[0 : 2 * sl, :] += dot(lhs, dzb[r])

    def over_replicas(src, dst, ssem, rsem):
        @pl.loop(1, dp)
        def _(k):
            remote(src, dst.at[my_dp], ssem, rsem, lax.rem(my_dp + k, dp), "dp").start()

        pltpu.make_async_copy(src, dst.at[my_dp], rsem).start()

    def middle():
        wait_for(w2r, pair_sem.at[11])
        dps[...] = jnp.sum(w2r[...].astype(F32), axis=0)
        over_replicas(dps, dpr, pair_sem.at[12], pair_sem.at[13])
        wait_for(bb, pair_sem.at[9])
        bt[...] = jnp.sum(bb[...], axis=0)
        over_replicas(bt, br, pair_sem.at[16], pair_sem.at[17])

    def late():
        wait_for(dpr, pair_sem.at[13])
        total = dpr[0]
        for k in range(1, dp):
            total = total + dpr[k]
        g2s[...] = total.astype(g2s.dtype)

        @pl.loop(1, half_n)
        def _(k):
            p = lax.rem(chip + k, half_n) * 2 + core
            remote(g2s, g2r.at[core, chip], pair_sem.at[18], pair_sem.at[19], p).start()

        pltpu.make_async_copy(g2s, g2r.at[core, chip], pair_sem.at[19]).start()

    dgather = Gather(dzb, dz_send, dz_recv)
    dgather.run(forward, weight, middle, late)
    w1s[...] = acc[0 : 2 * sl, :].astype(w1s.dtype)
    over_replicas(w1s, w1r, pair_sem.at[14], pair_sem.at[15])

    gather.finish()
    dgather.finish()
    wait_for(coli.at[pl.ds(0, n - 1)], pair_sem.at[0])
    wait_for(mv.at[0, pl.ds(0, n - 1)], pair_sem.at[2])
    wait_for(mv.at[1, pl.ds(0, n - 1)], pair_sem.at[4])
    wait_for(w2x, pair_sem.at[6])
    wait_for(bb.at[pl.ds(0, n - 1)], pair_sem.at[8])
    wait_for(w2r.at[pl.ds(0, half_n - 1)], pair_sem.at[10])
    wait_for(br, pair_sem.at[17])
    bias = br[0]
    for k in range(1, dp):
        bias = bias + br[k]
    gb1[...] = bias[:, :hid]
    gb2[...] = bias[:, hid:]
    wait_for(w1r, pair_sem.at[15])
    total = w1r[0].astype(F32)
    for k in range(1, dp):
        total = total + w1r[k].astype(F32)
    gw1[...] = total
    wait_for(g2r.at[core], pair_sem.at[19])
    last = remote(
        g2r.at[core], g2r.at[core], pair_sem.at[20], pair_sem.at[21], index(zz, xx, 1 - core)
    )
    last.start()
    wait_for(g2r.at[1 - core], pair_sem.at[21])
    for j in range(n):
        gw2[j * rows : (j + 1) * rows] = g2r[j % 2, j // 2].astype(F32)
    last.wait_send()
    wait_for(g2r.at[0, pl.ds(0, half_n - 1)], pair_sem.at[18])
    if dp > 1:
        wait_for(dpr.at[pl.ds(0, dp - 1)], pair_sem.at[12])
        wait_for(w1r.at[pl.ds(0, dp - 1)], pair_sem.at[14])
        wait_for(br.at[pl.ds(0, dp - 1)], pair_sem.at[16])


def hand_over(*refs):
    count = len(refs) // 2
    sems = refs[-1]
    copies = [pltpu.make_async_copy(refs[k], refs[count + k], sems.at[k]) for k in range(count)]
    for copy in copies:
        copy.start()
    for copy in copies:
        copy.wait()


def local(n, dp, x_feat, tiles_one, tile_cols, tile_counts, w_one, b_one, adj_two, w_two, b_two, cotangent):
    zs, xs = grid_of(n)
    sl, width = x_feat.shape[1:]
    tile = adj_two.shape[-1]
    slots = tiles_one.shape[1]
    hid = w_one.shape[2]
    rows = 2 * hid // n
    narrow = BF if rows % 16 == 0 else F32
    packed = slots * tile + 4 * sl
    vmem = pl.BlockSpec(memory_space=pltpu.VMEM)
    dma = pltpu.SemaphoreType.DMA
    results = pl.pallas_call(
        functools.partial(kernel, n, dp, zs, xs),
        out_shape=(
            jax.ShapeDtypeStruct((tile, hid), BF),
            jax.ShapeDtypeStruct((2 * sl, hid), F32),
            jax.ShapeDtypeStruct((1, hid), F32),
            jax.ShapeDtypeStruct((2 * hid, hid), F32),
            jax.ShapeDtypeStruct((1, hid), F32),
        ),
        in_specs=[pl.BlockSpec(memory_space=pltpu.HBM)] * 10,
        out_specs=(vmem,) * 5,
        scratch_shapes=[
            pltpu.VMEM((width // tile, sl, tile), BF),
            pltpu.VMEM((n, packed, tile), BF),
            pltpu.VMEM((2, n, sl, tile), BF),
            pltpu.VMEM((n, sl, tile), BF),
            pltpu.VMEM((n, tile, hid), BF),
            pltpu.VMEM((1, 128), jnp.int32),
            pltpu.VMEM((n, 1, 128), jnp.int32),
            pltpu.SMEM((n, 1, 128), jnp.int32),
            pltpu.VMEM((tile, hid), F32),
            pltpu.VMEM((max(tile, 2 * sl), hid), F32),
            pltpu.VMEM((2, n // 2, rows, hid), narrow),
            pltpu.VMEM((n // 2, rows, hid), narrow),
            pltpu.VMEM((n // 2, rows, hid), narrow),
            pltpu.VMEM((n // 2, rows, hid), narrow),
            pltpu.VMEM((rows, hid), narrow),
            pltpu.VMEM((2, n // 2, rows, hid), narrow),
            pltpu.VMEM((1, 2 * hid), F32),
            pltpu.VMEM((n, 1, 2 * hid), F32),
            pltpu.VMEM((1, 2 * hid), F32),
            pltpu.VMEM((dp, 1, 2 * hid), F32),
            pltpu.VMEM((rows, hid), F32),
            pltpu.VMEM((dp, rows, hid), F32),
            pltpu.VMEM((2 * sl, hid), BF),
            pltpu.VMEM((dp, 2 * sl, hid), BF),
            pltpu.VMEM((slots, tile, tile), BF),
            pltpu.SMEM((1, slots), jnp.int32),
            pltpu.SMEM((1, 1), jnp.int32),
            pltpu.VMEM((2, sl, hid), BF),
            pltpu.VMEM((1, hid), F32),
            pltpu.VMEM((tile, tile), BF),
            pltpu.VMEM((2, hid, hid), BF),
            pltpu.VMEM((1, hid), F32),
            pltpu.VMEM((tile, hid), BF),
            dma((2, n, xs + 2)),
            dma((2, n)),
            dma((2, n, xs + 2)),
            dma((2, n)),
            dma((22,)),
            dma((11,)),
        ],
        compiler_params=pltpu.CompilerParams(
            collective_id=0, has_side_effects=True, vmem_limit_bytes=63 * 1024 * 1024
        ),
    )(
        x_feat[0], tiles_one[0], tile_cols, tile_counts, w_one, b_one[None], adj_two[0], w_two,
        b_two[None], cotangent[0],
    )
    anywhere = pl.BlockSpec(memory_space=pl.ANY)
    out2, gw1, gb1, gw2, gb2 = pl.pallas_call(
        hand_over,
        out_shape=tuple(jax.ShapeDtypeStruct(r.shape, r.dtype) for r in results),
        in_specs=[anywhere] * 5,
        out_specs=(anywhere,) * 5,
        scratch_shapes=[dma((5,))],
        compiler_params=pltpu.CompilerParams(vmem_limit_bytes=63 * 1024 * 1024),
    )(*results)
    return (
        out2[None], gw1.reshape(2, sl, hid), gb1[0], gw2.reshape(2, hid, hid), gb2[0],
    )


def solution(mesh):
    in_specs = (
        P("dp", "feat", None),
        P("dp", "feat", None, None),
        P("dp", "feat"),
        P("dp", "feat"),
        P(None, "feat", None),
        P(),
        P("dp", "feat", None),
        P(),
        P(),
        P("dp", "feat", None),
    )
    out_specs = (P("dp", "feat", None), P(None, "feat", None), P(), P(), P())
    return jax.shard_map(
        functools.partial(local, mesh.shape["feat"], mesh.shape["dp"]),
        mesh=mesh, in_specs=in_specs, out_specs=out_specs, check_vma=False,
    )
```

```python
import functools
import math

import jax
import jax.numpy as jnp
from jax import lax
from jax.experimental import pallas as pl
from jax.experimental.pallas import tpu as pltpu
from jax.sharding import PartitionSpec as P

BF = jnp.bfloat16
F32 = jnp.float32


def dot(a, b, dims=((1,), (0,))):
    return lax.dot_general(a, b, (dims, ((), ())), preferred_element_type=F32)


def grid_of(n):
    x = max(math.isqrt(n // 4), 1)
    while (n // 2) % x:
        x -= 1
    return n // 2 // x, x


def kernel(
    n, dp, zs, xs,
    x_hbm, tiles_h, cols_h, counts_h, w1_h, b1_h, adj_h, w2_h, b2_h, cot_h,
    out2, gw1, gb1, gw2, gb2,
    xv, pack, mv, agg, dzb, colv, coli, cols_s, dh_s, acc,
    w2s, w2x, w2u, w2r, g2s, g2r, bs, bb, bt, br, dps, dpr, w1s, w1r,
    tiles, cols, counts, w1, b1, adj, w2, b2, cot,
    ag_send, ag_recv, dz_send, dz_recv, pair_sem, loc_sem,
):
    me = lax.axis_index("feat")
    my_dp = lax.axis_index("dp")
    core = lax.rem(me, 2)
    chip = lax.div(me, 2)
    xx = lax.rem(chip, xs)
    zz = lax.div(chip, xs)
    sl = w1.shape[1]
    tile = adj.shape[0]
    slots = tiles.shape[0]
    trows = slots * tile
    hid = w1.shape[2]
    half_w = hid // 2
    rows = w2s.shape[2]
    half_n = n // 2

    def index(z, x, c):
        return (z * xs + x) * 2 + c

    def remote(src, dst, ssem, rsem, peer, axis="feat"):
        return pltpu.make_async_remote_copy(
            src_ref=src, dst_ref=dst, send_sem=ssem, recv_sem=rsem,
            device_id={axis: peer}, device_id_type=pl.DeviceIdType.MESH,
        )

    def wait_for(ref, sem):
        pltpu.make_async_copy(ref, ref, sem).wait()

    early = [
        pltpu.make_async_copy(src, dst, loc_sem.at[2 + k])
        for k, (src, dst) in enumerate(
            [
                (cols_h, cols), (counts_h, counts), (tiles_h, tiles), (w1_h, w1), (cot_h, cot),
                (w2_h, w2), (adj_h, adj), (b1_h, b1), (b2_h, b2),
            ]
        )
    ]
    for copy in early:
        copy.start()
    barrier = pltpu.get_barrier_semaphore()

    @pl.loop(1, n)
    def _(k):
        pl.semaphore_signal(
            barrier, inc=1, device_id={"feat": lax.rem(me + k, n)}, device_id_type=pl.DeviceIdType.MESH
        )

    @pl.loop(1, dp)
    def _(k):
        pl.semaphore_signal(
            barrier, inc=1, device_id={"dp": lax.rem(my_dp + k, dp)}, device_id_type=pl.DeviceIdType.MESH
        )

    @pl.loop(0, xv.shape[0])
    def _(b):
        at = pl.multiple_of(b * tile, tile)
        pltpu.make_async_copy(x_hbm.at[:, pl.ds(at, tile)], xv.at[b], loc_sem.at[0]).start()

    for copy in early:
        copy.wait()
    count = counts[0, 0]
    lane = lax.broadcasted_iota(jnp.int32, (1, 128), 1)
    info = jnp.zeros((1, 128), jnp.int32)
    for s in range(slots):
        live = jnp.minimum(jnp.maximum(count - s, 0), 1).astype(F32)
        pack[me, s * tile : (s + 1) * tile, :] = (tiles[s].astype(F32) * live).astype(BF)
        info = jnp.where(lane == s, cols[0, s], info)
    colv[...] = info
    for k in range(2):
        for h in range(2):
            at = trows + (k * 2 + h) * sl
            pack[me, at : at + sl, :] = w1[k, :, h * half_w : (h + 1) * half_w]
    pl.semaphore_wait(barrier, n - 1 + dp - 1)

    class Gather:
        def __init__(self, buf, send, recv):
            self.buf, self.send, self.recv = buf, send, recv
            self.half = buf.shape[1] // 2

        def view(self, h, src):
            return self.buf.at[src, pl.ds(h * self.half, self.half), :]

        def copy(self, h, src, slot, peer):
            v = self.view(h, src)
            return remote(v, v, self.send.at[h, src, slot], self.recv.at[h, src], peer)

        def wait(self, h, src):
            wait_for(self.view(h, src), self.recv.at[h, src])

        def up(self, h, src, act):
            @pl.when(zz < zs - 1)
            def _():
                act(self.copy(h, src, 0, index(zz + 1, xx, core)))

        def down(self, h, src, act):
            @pl.when(zz > 0)
            def _():
                act(self.copy(h, src, 1, index(zz - 1, xx, core)))

        def across(self, h, src, act):
            for k in range(1, xs):
                act(self.copy(h, src, 1 + k, index(zz, lax.rem(xx + k, xs), core)))

        def sibling(self, h, src, act):
            act(self.copy(h, src, xs + 1, index(zz, xx, 1 - core)))

        def walk(self, act, first, arrive, ready, middle=lambda: None, late=lambda: None):
            def from_sibling(z, x):
                src = index(z, x, 1 - core)
                arrive(0, src)
                arrive(1, src)
                ready(src)

            for h in (1, 0):
                self.across(h, me, act)
                self.up(h, me, act)
                self.down(h, me, act)
                self.sibling(h, me, act)
            first()
            for k in range(1, xs):
                src = index(zz, lax.rem(xx + k, xs), core)
                arrive(1, src)
                self.up(1, src, act)
                self.down(1, src, act)
                self.sibling(1, src, act)
            ready(me)

            @pl.loop(1, zs)
            def _(k):
                @pl.when(zz - k >= 0)
                def _():
                    src = index(zz - k, xx, core)
                    arrive(0, src)
                    self.up(0, src, act)
                    self.across(0, src, act)
                    self.sibling(0, src, act)

                @pl.when(zz + k < zs)
                def _():
                    src = index(zz + k, xx, core)
                    arrive(0, src)
                    self.down(0, src, act)
                    self.across(0, src, act)
                    self.sibling(0, src, act)

                for j in range(xs):
                    other = lax.rem(xx + j, xs)

                    @pl.when(zz - k >= 0)
                    def _():
                        src = index(zz - k, other, core)
                        arrive(1, src)
                        self.up(1, src, act)
                        self.sibling(1, src, act)

                    @pl.when(zz + k < zs)
                    def _():
                        src = index(zz + k, other, core)
                        arrive(1, src)
                        self.down(1, src, act)
                        self.sibling(1, src, act)

                @pl.when(zz - k >= 0)
                def _():
                    ready(index(zz - k, xx, core))

                @pl.when(zz + k < zs)
                def _():
                    ready(index(zz + k, xx, core))

                @pl.when(zz - k + 1 >= 0)
                def _():
                    from_sibling(zz - k + 1, xx)

                @pl.when((zz + k - 1 < zs) & (k > 1))
                def _():
                    from_sibling(zz + k - 1, xx)

            middle()

            @pl.loop(0, zs)
            def _(k):
                z = lax.rem(zz + k, zs)
                for j in range(1, xs):
                    src = index(z, lax.rem(xx + j, xs), core)
                    arrive(0, src)
                    self.sibling(0, src, act)
                    ready(src)

            late()
            for z in ((zz - zs + 1), (zz + zs - 1)):
                @pl.when((z >= 0) & (z < zs))
                def _():
                    from_sibling(z, xx)

            @pl.loop(0, zs)
            def _(k):
                z = lax.rem(zz + k, zs)
                for j in range(1, xs):
                    from_sibling(z, lax.rem(xx + j, xs))

        def run(self, first, ready, *between):
            self.walk(lambda c: c.start(), first, self.wait, ready, *between)

        def finish(self):
            self.walk(lambda c: c.wait_send(), lambda: None, lambda h, s: None, lambda s: None)

    def features_out():
        @pl.loop(1, n)
        def _(k):
            p = lax.rem(me + k, n)
            remote(
                x_hbm.at[:, pl.ds(pl.multiple_of(p * tile, tile), tile)], mv.at[0, me],
                pair_sem.at[2], pair_sem.at[3], p,
            ).start()

        at = pl.multiple_of(me * tile, tile)
        pltpu.make_async_copy(x_hbm.at[:, pl.ds(at, tile)], mv.at[0, me], pair_sem.at[3]).start()

    @pl.loop(1, n)
    def _(k):
        remote(colv, coli.at[me], pair_sem.at[0], pair_sem.at[1], lax.rem(me + k, n)).start()

    pltpu.make_async_copy(colv, coli.at[me], pair_sem.at[1]).start()

    def before_relay():
        features_out()
        bs[:, hid:] = jnp.sum(cot[...].astype(F32), axis=0, keepdims=True)
        dagg = dot(cot[...], w2[1], ((1,), (1,))).astype(BF)
        dh = dot(cot[...], w2[0], ((1,), (1,)))
        dh_s[...] = dh + dot(adj[...], dagg, ((0,), (0,)))
        wait_for(coli, pair_sem.at[1])
        to_smem = pltpu.make_async_copy(coli, cols_s, loc_sem.at[1])
        to_smem.start()
        to_smem.wait()
        wait_for(xv, loc_sem.at[0])

    gather = Gather(pack, ag_send, ag_recv)

    def aggregate(r):
        total = jnp.zeros((sl, tile), F32)
        for s in range(slots):
            total += dot(xv[cols_s[r, 0, s]], pack[r, s * tile : (s + 1) * tile, :], ((1,), (1,)))
        agg[r] = total.astype(BF)

        @pl.when(r != me)
        def _():
            remote(agg.at[r], mv.at[1, me], pair_sem.at[4], pair_sem.at[5], r).start()

        @pl.when(r == me)
        def _():
            pltpu.make_async_copy(agg.at[r], mv.at[1, me], pair_sem.at[5]).start()

    gather.run(before_relay, aggregate)

    def project(k):
        at = trows + k * 2 * sl
        w = jnp.concatenate(
            [
                pack[:, at + h * sl : at + (h + 1) * sl, :].reshape(n * sl, half_w)
                for h in range(2)
            ],
            axis=1,
        )
        return dot(mv[k].reshape(n * sl, tile), w, ((0,), (0,)))

    wait_for(mv.at[0], pair_sem.at[3])
    acc[...] = project(0) + b1[...]
    wait_for(mv.at[1], pair_sem.at[5])
    z = acc[...] + project(1)
    sig = 1.0 / (1.0 + jnp.exp(-z))
    h_one = (z * sig).astype(BF)
    dz = (dh_s[...] * sig * (1.0 + z * (1.0 - sig))).astype(BF)
    dzb[me] = dz
    bs[:, :hid] = jnp.sum(dz.astype(F32), axis=0, keepdims=True)

    def forward():
        agg_two = dot(adj[...], h_one).astype(BF)
        g0 = dot(h_one, cot[...], ((0,), (0,)))
        g1 = dot(agg_two, cot[...], ((0,), (0,)))
        for j in range(n):
            g = (g0, g1)[j // half_n]
            at = (j % half_n) * rows
            w2s[j % 2, j // 2] = g[at : at + rows].astype(w2s.dtype)
        remote(w2s.at[1 - core], w2x, pair_sem.at[6], pair_sem.at[7], index(zz, xx, 1 - core)).start()

        @pl.loop(1, n)
        def _(k):
            remote(bs, bb.at[me], pair_sem.at[8], pair_sem.at[9], lax.rem(me + k, n)).start()

        pltpu.make_async_copy(bs, bb.at[me], pair_sem.at[9]).start()
        z2 = dot(h_one, w2[0]) + dot(agg_two, w2[1]) + b2[...]
        out2[...] = z2.astype(BF)
        wait_for(w2x, pair_sem.at[7])
        w2u[...] = (w2s[core].astype(F32) + w2x[...].astype(F32)).astype(w2u.dtype)

        @pl.loop(1, half_n)
        def _(k):
            p = lax.rem(chip + k, half_n)
            remote(w2u.at[p], w2r.at[chip], pair_sem.at[10], pair_sem.at[11], p * 2 + core).start()

        pltpu.make_async_copy(w2u.at[chip], w2r.at[chip], pair_sem.at[11]).start()

    acc[...] = jnp.zeros_like(acc)

    def weight(r):
        lhs = jnp.concatenate([xv[r], agg[r]], axis=0)
        acc[0 : 2 * sl, :] += dot(lhs, dzb[r])

    def over_replicas(src, dst, ssem, rsem):
        @pl.loop(1, dp)
        def _(k):
            remote(src, dst.at[my_dp], ssem, rsem, lax.rem(my_dp + k, dp), "dp").start()

        pltpu.make_async_copy(src, dst.at[my_dp], rsem).start()

    def middle():
        wait_for(w2r, pair_sem.at[11])
        dps[...] = jnp.sum(w2r[...].astype(F32), axis=0)
        over_replicas(dps, dpr, pair_sem.at[12], pair_sem.at[13])
        wait_for(bb, pair_sem.at[9])
        bt[...] = jnp.sum(bb[...], axis=0)
        over_replicas(bt, br, pair_sem.at[16], pair_sem.at[17])

    def late():
        wait_for(dpr, pair_sem.at[13])
        total = dpr[0]
        for k in range(1, dp):
            total = total + dpr[k]
        g2s[...] = total.astype(g2s.dtype)

        @pl.loop(1, half_n)
        def _(k):
            p = lax.rem(chip + k, half_n) * 2 + core
            remote(g2s, g2r.at[core, chip], pair_sem.at[18], pair_sem.at[19], p).start()

        pltpu.make_async_copy(g2s, g2r.at[core, chip], pair_sem.at[19]).start()

    dgather = Gather(dzb, dz_send, dz_recv)
    dgather.run(forward, weight, middle, late)
    w1s[...] = acc[0 : 2 * sl, :].astype(w1s.dtype)
    over_replicas(w1s, w1r, pair_sem.at[14], pair_sem.at[15])

    gather.finish()
    dgather.finish()
    wait_for(coli.at[pl.ds(0, n - 1)], pair_sem.at[0])
    wait_for(mv.at[0, pl.ds(0, n - 1)], pair_sem.at[2])
    wait_for(mv.at[1, pl.ds(0, n - 1)], pair_sem.at[4])
    wait_for(w2x, pair_sem.at[6])
    wait_for(bb.at[pl.ds(0, n - 1)], pair_sem.at[8])
    wait_for(w2r.at[pl.ds(0, half_n - 1)], pair_sem.at[10])
    wait_for(br, pair_sem.at[17])
    bias = br[0]
    for k in range(1, dp):
        bias = bias + br[k]
    gb1[...] = bias[:, :hid]
    gb2[...] = bias[:, hid:]
    wait_for(w1r, pair_sem.at[15])
    total = w1r[0].astype(F32)
    for k in range(1, dp):
        total = total + w1r[k].astype(F32)
    gw1[...] = total
    wait_for(g2r.at[core], pair_sem.at[19])
    last = remote(
        g2r.at[core], g2r.at[core], pair_sem.at[20], pair_sem.at[21], index(zz, xx, 1 - core)
    )
    last.start()
    wait_for(g2r.at[1 - core], pair_sem.at[21])
    for j in range(n):
        gw2[j * rows : (j + 1) * rows] = g2r[j % 2, j // 2].astype(F32)
    last.wait_send()
    wait_for(g2r.at[0, pl.ds(0, half_n - 1)], pair_sem.at[18])
    if dp > 1:
        wait_for(dpr.at[pl.ds(0, dp - 1)], pair_sem.at[12])
        wait_for(w1r.at[pl.ds(0, dp - 1)], pair_sem.at[14])
        wait_for(br.at[pl.ds(0, dp - 1)], pair_sem.at[16])


def local(n, dp, x_feat, tiles_one, tile_cols, tile_counts, w_one, b_one, adj_two, w_two, b_two, cotangent):
    zs, xs = grid_of(n)
    sl, width = x_feat.shape[1:]
    tile = adj_two.shape[-1]
    slots = tiles_one.shape[1]
    hid = w_one.shape[2]
    rows = 2 * hid // n
    narrow = BF if rows % 16 == 0 else F32
    packed = slots * tile + 4 * sl
    vmem = pl.BlockSpec(memory_space=pltpu.VMEM)
    dma = pltpu.SemaphoreType.DMA
    out2, gw1, gb1, gw2, gb2 = pl.pallas_call(
        functools.partial(kernel, n, dp, zs, xs),
        out_shape=(
            jax.ShapeDtypeStruct((tile, hid), BF),
            jax.ShapeDtypeStruct((2 * sl, hid), F32),
            jax.ShapeDtypeStruct((1, hid), F32),
            jax.ShapeDtypeStruct((2 * hid, hid), F32),
            jax.ShapeDtypeStruct((1, hid), F32),
        ),
        in_specs=[pl.BlockSpec(memory_space=pltpu.HBM)] * 10,
        out_specs=(vmem,) * 5,
        scratch_shapes=[
            pltpu.VMEM((width // tile, sl, tile), BF),
            pltpu.VMEM((n, packed, tile), BF),
            pltpu.VMEM((2, n, sl, tile), BF),
            pltpu.VMEM((n, sl, tile), BF),
            pltpu.VMEM((n, tile, hid), BF),
            pltpu.VMEM((1, 128), jnp.int32),
            pltpu.VMEM((n, 1, 128), jnp.int32),
            pltpu.SMEM((n, 1, 128), jnp.int32),
            pltpu.VMEM((tile, hid), F32),
            pltpu.VMEM((max(tile, 2 * sl), hid), F32),
            pltpu.VMEM((2, n // 2, rows, hid), narrow),
            pltpu.VMEM((n // 2, rows, hid), narrow),
            pltpu.VMEM((n // 2, rows, hid), narrow),
            pltpu.VMEM((n // 2, rows, hid), narrow),
            pltpu.VMEM((rows, hid), narrow),
            pltpu.VMEM((2, n // 2, rows, hid), narrow),
            pltpu.VMEM((1, 2 * hid), F32),
            pltpu.VMEM((n, 1, 2 * hid), F32),
            pltpu.VMEM((1, 2 * hid), F32),
            pltpu.VMEM((dp, 1, 2 * hid), F32),
            pltpu.VMEM((rows, hid), F32),
            pltpu.VMEM((dp, rows, hid), F32),
            pltpu.VMEM((2 * sl, hid), BF),
            pltpu.VMEM((dp, 2 * sl, hid), BF),
            pltpu.VMEM((slots, tile, tile), BF),
            pltpu.SMEM((1, slots), jnp.int32),
            pltpu.SMEM((1, 1), jnp.int32),
            pltpu.VMEM((2, sl, hid), BF),
            pltpu.VMEM((1, hid), F32),
            pltpu.VMEM((tile, tile), BF),
            pltpu.VMEM((2, hid, hid), BF),
            pltpu.VMEM((1, hid), F32),
            pltpu.VMEM((tile, hid), BF),
            dma((2, n, xs + 2)),
            dma((2, n)),
            dma((2, n, xs + 2)),
            dma((2, n)),
            dma((22,)),
            dma((11,)),
        ],
        compiler_params=pltpu.CompilerParams(
            collective_id=0, has_side_effects=True, vmem_limit_bytes=63 * 1024 * 1024
        ),
    )(
        x_feat[0], tiles_one[0], tile_cols, tile_counts, w_one, b_one[None], adj_two[0], w_two,
        b_two[None], cotangent[0],
    )
    return (
        out2[None], gw1.reshape(2, sl, hid), gb1[0], gw2.reshape(2, hid, hid), gb2[0],
    )


def solution(mesh):
    in_specs = (
        P("dp", "feat", None),
        P("dp", "feat", None, None),
        P("dp", "feat"),
        P("dp", "feat"),
        P(None, "feat", None),
        P(),
        P("dp", "feat", None),
        P(),
        P(),
        P("dp", "feat", None),
    )
    out_specs = (P("dp", "feat", None), P(None, "feat", None), P(), P(), P())
    return jax.shard_map(
        functools.partial(local, mesh.shape["feat"], mesh.shape["dp"]),
        mesh=mesh, in_specs=in_specs, out_specs=out_specs, check_vma=False,
    )
```
